256 devices in a mesh: ctx: 32 (over z, x), head: 8 (over y, core).
Axes of the slice: x: 4, y: 4, z: 8, core: 2. Of those that a mesh axis runs over, the one named last changes fastest.
Arguments:
- tokens: bfloat16 [4096, 2048], P('ctx'), may hold values from -6 to 6
- doc_lengths: int32 [16], replicated, may hold values from 1 to 2048, 4096 in all
- w_query: bfloat16 [2048, 2048], P(None, 'head'), may hold values from -0.125 to 0.125
- w_key: bfloat16 [2048, 2048], P(None, 'head'), may hold values from -0.125 to 0.125
- w_value: bfloat16 [2048, 4096], P(None, 'head'), may hold values from -0.125 to 0.125
- w_gate: bfloat16 [2048, 4096], P(None, 'head'), may hold values from -0.125 to 0.125
- conv_query: bfloat16 [4, 2048], P(None, 'head'), may hold values from -3 to 3
- conv_key: bfloat16 [4, 2048], P(None, 'head'), may hold values from -3 to 3
- conv_value: bfloat16 [4, 4096], P(None, 'head'), may hold values from -3 to 3
- beta_logit: float32 [32, 4096], P('head', 'ctx'), may hold values from -6 to 6
- decay_logit: float32 [32, 4096], P('head', 'ctx'), may hold values from -3 to 4096
- a_log: float32 [32], P('head')
- w_output: bfloat16 [4096, 2048], P('head'), may hold values from -0.09375 to 0.09375
Outputs:
- mixed: bfloat16 [4096, 2048], P(('ctx', 'head'))
The draws below stay inside these ranges and needn't reach their ends.
Inputs may be any that keep to these rules, and one draw needn't show every extreme that they name: `doc_lengths`: lengths of the documents in packing order; they sum to 4096, and the longest has exactly 2048 tokens.
All inputs are finite; a program needn't handle non-finite values.
Results may differ from the reference program's by a relative error of at most 0.023.
Values may be sent and summed in bfloat16 or wider, within the bound.
A program may use at most 128 MiB of HBM per device.

```python
import math
import jax
import jax.numpy as jnp
import numpy as np
from jax import lax

D = 2048
NV = 32
NK = 16
DK = 128
DV = 128
CONVK = 4
STRETCH = 64
DOCS = 16
TOK_DEV = 128
PACKED_TOKENS = 4096
KEYDIM = 2048
VALDIM = 4096
N_HEAD = 8


def head_rates(key):
    inner_product = jax.random.fold_in(key, 101)
    pick_key, slow_key, fast_key = jax.random.split(inner_product, 3)
    slow_heads = jax.random.bernoulli(pick_key, 0.5, (NV,))
    slow_rate = jax.random.uniform(slow_key, (NV,), jnp.float32, 0.5, 2.0) / PACKED_TOKENS
    fast_rate = jnp.exp(jax.random.uniform(fast_key, (NV,), jnp.float32, jnp.log(0.025), jnp.log(0.05)))
    return jnp.where(slow_heads, slow_rate, fast_rate)


def draw_a_log(key, part):
    return jnp.log(head_rates(key))


def draw_decay_logit(key, part):
    decay_factors = head_rates(key)
    inner_product = jax.random.fold_in(key, 202)
    root_random_key, block_random_key, spike_random_key = jax.random.split(inner_product, 3)
    base_random_field = jnp.clip(0.5 * jax.random.normal(root_random_key, (NV, PACKED_TOKENS), jnp.float32), -1.5, 1.5)
    block_shift = jax.random.uniform(block_random_key, (NV, PACKED_TOKENS // TOK_DEV), jnp.float32, -1.0, 1.0)
    base_random_field = base_random_field + jnp.repeat(block_shift, TOK_DEV, axis=1)
    spike_positions = jax.random.randint(spike_random_key, (6,), 0, PACKED_TOKENS)
    spike_mask = jnp.any(jnp.arange(PACKED_TOKENS)[None, :] == spike_positions[:, None], axis=0)
    return jnp.where(spike_mask[None, :], (0.4 / decay_factors)[:, None], base_random_field)


def steps_of(own_key, dims, shards, low, top_value):
    factor_of = 1.0
    for position, shards_of in shards:
        draws = jax.random.uniform(jax.random.fold_in(jax.random.fold_in(own_key, 6), position), (shards_of,), jnp.float32, low / len(shards), top_value / len(shards))
        factor_of = factor_of * jnp.repeat(jnp.exp(draws), dims[position] // shards_of).reshape((-1,) + (1,) * (len(dims) - 1 - position))
    return factor_of


def length_profile(amount, total, most, skew):
    weights = [(1 << 20) // math.isqrt(rank ** skew) + 1 for rank in range(2, amount + 1)]
    spare, counts = total - most - (amount - 1), [1] * (amount - 1)
    while spare > 0:
        movable = [i for i in range(amount - 1) if counts[i] < most]
        mass, budget = sum([weights[i] for i in movable]), spare
        for i in movable:
            extra = min(most - counts[i], max(1, budget * weights[i] // mass), spare)
            counts[i] = counts[i] + extra
            spare = spare - extra
    return np.array([most] + counts)


def uneven_parts(rng, amount, total, most, slope):
    if amount == 2:
        one = jax.random.randint(rng, (), max(1, total - most), min(most, total - 1) + 1)
        return jnp.stack([one, total - one])
    lengths = jnp.asarray(length_profile(amount, total, most, slope), jnp.int32)
    couples = (amount - 1) // 2
    giver, sink = lengths[1:1 + 2 * couples:2], lengths[2:2 + 2 * couples:2]
    margin = jnp.minimum(giver - 1, most - sink)
    passed = jax.random.randint(jax.random.fold_in(rng, 1), (couples,), 0, 1 << 20) % (margin + 1)
    lengths = lengths.at[1:1 + 2 * couples:2].set(giver - passed).at[2:2 + 2 * couples:2].set(sink + passed)
    return lengths[jax.random.permutation(jax.random.fold_in(rng, 2), amount)]


def gaussian(rng, shape, scale, bound, cuts=(), kind=jnp.bfloat16):
    values = jax.random.normal(rng, shape, jnp.float32) * scale
    if len(cuts) > 0:
        values = steps_of(rng, shape, cuts, -0.22, 0.18) * values
    return jnp.clip(values, min=-bound, max=bound).astype(kind)


def setup_inputs(seed: int = 0) -> dict:
    seeds = jax.random.split(jax.random.key(seed), 14)
    tokens = gaussian(seeds[0], (PACKED_TOKENS, D), 1.0, 6.0, ((0, 32),))
    doc_lengths = uneven_parts(seeds[1], DOCS, PACKED_TOKENS, PACKED_TOKENS // 2, 2).astype(jnp.int32)
    w_query = gaussian(seeds[2], (D, KEYDIM), D ** -0.5, 0.125, ((1, 8),))
    w_key = gaussian(seeds[3], (D, KEYDIM), D ** -0.5, 0.125, ((1, 8),))
    w_value = gaussian(seeds[4], (D, VALDIM), D ** -0.5, 0.125, ((1, 8),))
    w_gate = gaussian(seeds[5], (D, VALDIM), D ** -0.5, 0.125, ((1, 8),))
    conv_query = gaussian(seeds[6], (CONVK, KEYDIM), CONVK ** -0.5, 3.0, ((1, 8),))
    conv_key = gaussian(seeds[7], (CONVK, KEYDIM), CONVK ** -0.5, 3.0, ((1, 8),))
    conv_value = gaussian(seeds[8], (CONVK, VALDIM), CONVK ** -0.5, 3.0, ((1, 8),))
    beta_logit = gaussian(seeds[9], (NV, PACKED_TOKENS), 1.0, 6.0, ((0, 8), (1, 32)), jnp.float32)
    decay_logit = draw_decay_logit(jax.random.fold_in(seeds[13], 71), 0)
    a_log = draw_a_log(jax.random.fold_in(seeds[13], 71), 0)
    w_output = gaussian(seeds[12], (VALDIM, D), VALDIM ** -0.5, 0.09375, ((0, 8),))
    return {"tokens": tokens, "doc_lengths": doc_lengths, "w_query": w_query, "w_key": w_key, "w_value": w_value, "w_gate": w_gate, "conv_query": conv_query, "conv_key": conv_key, "conv_value": conv_value, "beta_logit": beta_logit, "decay_logit": decay_logit, "a_log": a_log, "w_output": w_output}


HIGHP = lax.Precision.HIGHEST

def batched_heads(form, left_op, right_op):
    return jnp.einsum(form, left_op, right_op, precision=HIGHP)

def doc_tables(doc_lengths, positions):
    doc_ends = jnp.cumsum(doc_lengths).astype(jnp.int32)
    offsets = (doc_ends - doc_lengths).astype(jnp.int32)
    starts = jnp.any(positions[:, None] == offsets[None, :], axis=1)
    doc_ids = lax.optimization_barrier(jnp.sum((offsets[None, 1:] <= positions[:, None]).astype(jnp.int32), axis=1)).astype(jnp.int32)
    return (starts, doc_ids)

def short_conv(extended, weight, positions, doc_ids):
    tap_count = weight.shape[0]
    row_count = extended.shape[0] - tap_count + 1
    here_docs = doc_ids[tap_count - 1:]
    running_sum = jnp.zeros((row_count, extended.shape[1]), jnp.float32)
    for tap_index in range(tap_count):
        window = extended[tap_index:tap_index + row_count].astype(jnp.float32)
        keep_rows = (doc_ids[tap_index:tap_index + row_count] == here_docs) & (positions[tap_index:tap_index + row_count] >= 0)
        running_sum = running_sum + jnp.where(keep_rows[:, None], weight[tap_index].astype(jnp.float32)[None, :] * window, 0.0)
    return jax.nn.silu(running_sum)

def unit_norm(field):
    return field * lax.rsqrt(lax.optimization_barrier(jnp.sum(field * field, axis=-1, keepdims=True)) + 1e-06)

def stretch_parts(query_matrix_rows, key_matrix_rows, value_rows, beta_rate, log_decay, doc_ids, prev_doc):
    span_len = query_matrix_rows.shape[1]
    index_line = jnp.arange(span_len, dtype=jnp.int32)
    lower_incl = index_line[:, None] >= index_line[None, :]
    tri_ones = lower_incl.astype(jnp.float32)
    cumulative = batched_heads('ij,hj->hi', tri_ones, log_decay)
    same_doc = (doc_ids[:, None] == doc_ids[None, :]) & lower_incl
    decay_gap = jnp.where(same_doc[None], cumulative[:, :, None] - cumulative[:, None, :], 0.0)
    decay_mat = jnp.where(same_doc[None], jnp.exp(decay_gap), 0.0)
    kept_flag = (doc_ids == prev_doc).astype(jnp.float32)
    per_head_decay = jnp.exp(cumulative) * kept_flag[None, :]
    key_gram = batched_heads('hik,hjk->hij', key_matrix_rows, key_matrix_rows)
    strict_low = index_line[:, None] > index_line[None, :]
    lower_part = jnp.where(strict_low[None], beta_rate[:, :, None] * decay_mat * key_gram, 0.0)
    system = lower_part + jnp.eye(span_len, dtype=jnp.float32)[None]
    right_side = jnp.concatenate([beta_rate[:, :, None] * value_rows, (beta_rate * per_head_decay)[:, :, None] * key_matrix_rows], axis=2)
    solved = jax.scipy.linalg.solve_triangular(system, right_side, lower=True, unit_diagonal=True)
    value_width = value_rows.shape[2]
    state_update = solved[:, :, :value_width]
    weighted_values = solved[:, :, value_width:]
    attention_scores = decay_mat * batched_heads('hik,hjk->hij', query_matrix_rows, key_matrix_rows)
    final_row = decay_mat[:, span_len - 1, :]
    return (per_head_decay, state_update, weighted_values, attention_scores, final_row)

def stretch_out(stretch_terms, entry_state, query_matrix_rows, key_matrix_rows):
    per_head_decay, state_update, weighted_values, attention_scores, final_row = stretch_terms
    corrected_values = state_update - batched_heads('xyz,xzr->xyr', weighted_values, entry_state)
    segment_output = per_head_decay[:, :, None] * batched_heads('xyz,xzr->xyr', query_matrix_rows, entry_state) + batched_heads('uyc,ucb->uyb', attention_scores, corrected_values)
    updated_state = per_head_decay[:, -1][:, None, None] * entry_state + batched_heads('uyf,uyz->ufz', final_row[:, :, None] * key_matrix_rows, corrected_values)
    return (segment_output, updated_state)

def blocks_three(field, stretch_count, stretch_len):
    return jnp.transpose(field.reshape(field.shape[0], stretch_count, stretch_len, field.shape[2]), (1, 0, 2, 3))

def blocks_two(field, stretch_count, stretch_len):
    return jnp.transpose(field.reshape(field.shape[0], stretch_count, stretch_len), (1, 0, 2))

def reference(tokens, doc_lengths, w_query, w_key, w_value, w_gate, conv_query, conv_key, conv_value, beta_logit, decay_logit, a_log, w_output):
    conv_lag = CONVK - 1
    positions = jnp.arange(-conv_lag, PACKED_TOKENS, dtype=jnp.int32)
    starts, doc_ids = doc_tables(doc_lengths, positions)
    own_docs = doc_ids[conv_lag:]
    own_starts = starts[conv_lag:].astype(jnp.int32)
    stretch_count = PACKED_TOKENS // STRETCH
    stretch_docs = own_docs.reshape(stretch_count, STRETCH)
    prev_docs = (stretch_docs[:, 0] - own_starts.reshape(stretch_count, STRETCH)[:, 0]).astype(jnp.int32)
    key_group = NK // N_HEAD
    value_group = NV // N_HEAD
    ratio_heads = NV // NK
    key_cols = key_group * DK
    value_cols = value_group * DV

    def run_group(running_sum, group_index):

        def columns(weight, width_cols):
            return lax.dynamic_slice_in_dim(weight, (group_index * width_cols).astype(jnp.int32), width_cols, 1)

        def head_rows(field):
            return lax.dynamic_slice_in_dim(field, (group_index * value_group).astype(jnp.int32), value_group, 0)
        proj_query = jnp.dot(tokens.astype(jnp.float32), columns(w_query, key_cols).astype(jnp.float32), preferred_element_type=jnp.float32).astype(jnp.bfloat16)
        proj_key = jnp.dot(tokens.astype(jnp.float32), columns(w_key, key_cols).astype(jnp.float32), preferred_element_type=jnp.float32).astype(jnp.bfloat16)
        proj_value = jnp.dot(tokens.astype(jnp.float32), columns(w_value, value_cols).astype(jnp.float32), preferred_element_type=jnp.float32).astype(jnp.bfloat16)
        proj_gate = jnp.dot(tokens.astype(jnp.float32), columns(w_gate, value_cols).astype(jnp.float32), preferred_element_type=jnp.float32).astype(jnp.bfloat16)
        zero_keys = jnp.zeros((conv_lag, key_cols), jnp.bfloat16)
        zero_values = jnp.zeros((conv_lag, value_cols), jnp.bfloat16)
        conv_q = short_conv(jnp.concatenate([zero_keys, proj_query], 0), columns(conv_query, key_cols), positions, doc_ids)
        conv_k = short_conv(jnp.concatenate([zero_keys, proj_key], 0), columns(conv_key, key_cols), positions, doc_ids)
        conv_v = short_conv(jnp.concatenate([zero_values, proj_value], 0), columns(conv_value, value_cols), positions, doc_ids)
        query_heads = unit_norm(conv_q.reshape(PACKED_TOKENS, key_group, DK)) * DK ** (-0.5)
        key_heads = unit_norm(conv_k.reshape(PACKED_TOKENS, key_group, DK))
        query_heads = jnp.repeat(jnp.transpose(query_heads, (1, 0, 2)), ratio_heads, axis=0)
        key_heads = jnp.repeat(jnp.transpose(key_heads, (1, 0, 2)), ratio_heads, axis=0)
        value_heads = jnp.transpose(conv_v.reshape(PACKED_TOKENS, value_group, DV), (1, 0, 2))
        beta_rate = jax.nn.sigmoid(head_rows(beta_logit))
        decay_factors = jnp.exp(head_rows(a_log))
        log_decay = -decay_factors[:, None] * jax.nn.softplus(head_rows(decay_logit))
        stretch_inputs = (blocks_three(query_heads, stretch_count, STRETCH), blocks_three(key_heads, stretch_count, STRETCH), blocks_three(value_heads, stretch_count, STRETCH), blocks_two(beta_rate, stretch_count, STRETCH), blocks_two(log_decay, stretch_count, STRETCH), stretch_docs, prev_docs)

        def advance(entry_state, inputs):
            query_matrix_rows, key_matrix_rows, value_rows, beta_rows, decay_rows, docs_here, prev_here = inputs
            stretch_terms = stretch_parts(query_matrix_rows, key_matrix_rows, value_rows, beta_rows, decay_rows, docs_here, prev_here)
            segment_output, updated_state = stretch_out(stretch_terms, entry_state, query_matrix_rows, key_matrix_rows)
            return (updated_state, segment_output)
        _, outputs = lax.scan(advance, jnp.zeros((value_group, DK, DV), jnp.float32), stretch_inputs)
        outputs = jnp.transpose(outputs, (0, 2, 1, 3)).reshape(PACKED_TOKENS, value_group, DV)
        gate_heads = proj_gate.reshape(PACKED_TOKENS, value_group, DV).astype(jnp.float32)
        normed = outputs * lax.rsqrt(lax.optimization_barrier(jnp.mean(outputs * outputs, axis=-1, keepdims=True)) + 1e-06)
        gated_rows = (normed * jax.nn.silu(gate_heads)).astype(jnp.bfloat16).reshape(PACKED_TOKENS, value_cols)
        out_rows = lax.dynamic_slice_in_dim(w_output, (group_index * value_cols).astype(jnp.int32), value_cols, 0)
        partial_sum = jnp.dot(gated_rows.astype(jnp.float32), out_rows.astype(jnp.float32), preferred_element_type=jnp.float32)
        rounded = lax.optimization_barrier(partial_sum.astype(jnp.bfloat16)).astype(jnp.float32)
        return (running_sum + rounded, None)
    running_sum, _ = lax.scan(run_group, jnp.zeros((PACKED_TOKENS, D), jnp.float32), jnp.arange(N_HEAD, dtype=jnp.int32))
    return running_sum.astype(jnp.bfloat16)
```

```python
import jax
import jax.numpy as jnp
from jax import lax
from jax.experimental import pallas as pl
from jax.experimental.pallas import tpu as pltpu
from jax.sharding import PartitionSpec as P

MESH = pl.DeviceIdType.MESH
F32 = jnp.float32
BF = jnp.bfloat16
T = 128
W = 128
NX = 4
NZ = 8
NY = 4
HV = 4
HK = 2
DOCS = 16
SUB = 16
NCH = 2
D = 2048


def mm(a, b):
    return jnp.dot(a, b, preferred_element_type=F32)


def mm_t(a, b):
    return lax.dot_general(a, b, (((1,), (1,)), ((), ())), preferred_element_type=F32)


def iota(shape, dim):
    return lax.broadcasted_iota(jnp.int32, shape, dim)


def kernel(
    tok_h, doc_h, wq_h, wk_h, wv_h, wg_h, cq_h, ck_h, cv_h, bl_h, dl_h, al_h, wo_h,
    out_ref,
    tok, wq, wk, wv, wg, wo, cq, ck, cv, bl, dl, doc_s, al_s,
    pk, pq, pv, hk, hq, hv, ext, sc8, dm, bdm, dcol, bcol, pick,
    sg, psend, pbuf, o1, qt, qs, rb_mu, rb_u, ssend, srecv, yb, pm, rc, s2, ry,
    lsem, ss, rs_halo, rs_x, rs_z, rs_b, rs_r, rs_c, rs_y,
):
    c = lax.axis_index("ctx")
    hd = lax.axis_index("head")
    z, x = c // NX, c % NX
    y, co = hd // 2, hd % 2

    def at_zx(dz, dx):
        return (lax.rem(z + dz + NZ, NZ) * NX + lax.rem(x + dx, NX), hd)

    def at_y(dy):
        return (c, lax.rem(y + dy, NY) * 2 + co)

    partner = (c, y * 2 + 1 - co)

    def load(i, src, dst):
        cp = pltpu.make_async_copy(src, dst, lsem.at[i])
        cp.start()
        return cp

    l_doc = load(0, doc_h, doc_s)
    l_al = load(1, al_h, al_s)
    l_bl = load(2, bl_h, bl)
    l_dl = load(3, dl_h, dl)
    l_tok = load(4, tok_h, tok)
    l_wk = load(5, wk_h, wk)
    l_wq = load(6, wq_h, wq)
    l_wv = load(7, wv_h, wv)
    l_ck = load(8, ck_h, ck)
    l_cq = load(9, cq_h, cq)
    l_cv = load(10, cv_h, cv)
    l_wg = load(11, wg_h, wg)
    l_wo = load(12, wo_h, wo)

    barrier = pltpu.get_barrier_semaphore()
    sources = [at_zx(0, d) for d in (1, 2, 3)]
    sources += [at_zx(-1, d) for d in range(NX)]
    sources += [at_zx(-3, 0), partner]
    sources += [at_y(d) for d in (1, 2, 3)]
    for dev in sources:
        pl.semaphore_signal(barrier, inc=1, device_id=dev, device_id_type=MESH)

    l_doc.wait()
    l_al.wait()
    l_bl.wait()
    l_dl.wait()
    base = c * T
    offs = []
    total = jnp.int32(0)
    for j in range(DOCS):
        offs.append(total)
        total = total + doc_s[j]
    row = iota((T, T), 0)
    lane = iota((T, T), 1)
    start = jnp.zeros((T, T), jnp.int32)
    start_last = jnp.int32(0)
    for j in range(1, DOCS):
        start = jnp.where(offs[j] <= row + base, offs[j], start)
        start_last = jnp.where(offs[j] <= base + T - 1, offs[j], start_last)
    age = row + base - start
    kept = start < base
    lower = (lane <= row) & (base + lane >= start)
    strict = lane < row
    dlv = dl[...]
    soft = jnp.maximum(dlv, 0.0) + jnp.log(1.0 + jnp.exp(-jnp.abs(dlv)))
    r4 = iota((HV, T), 0)
    rate = jnp.where(r4 == 0, al_s[0], jnp.where(r4 == 1, al_s[1], jnp.where(r4 == 2, al_s[2], al_s[3])))
    sc8[0:HV] = -jnp.exp(rate) * soft
    sc8[HV : 2 * HV] = 1.0 / (1.0 + jnp.exp(-bl[...]))
    both = sc8[...]
    upper = (row <= lane).astype(F32)
    cum = jnp.dot(both, upper, preferred_element_type=F32, precision=lax.Precision.HIGHEST)
    both = jnp.where(iota((2 * HV, T), 0) < HV, cum, both)
    cols = jnp.transpose(both)
    f_row, d_last = [], []
    for h in range(HV):
        gcol = jnp.broadcast_to(cols[:, h : h + 1], (T, T))
        grow = both[h : h + 1, :]
        decay = jnp.exp(jnp.where(lower, gcol - grow, -1e30))
        beta = jnp.broadcast_to(cols[:, HV + h : HV + h + 1], (T, T))
        into = jnp.where(kept, jnp.exp(gcol), 0.0)
        dm[h] = decay
        bdm[h] = jnp.where(strict, decay * beta, 0.0)
        dcol[h] = into
        bcol[h] = beta
        f_row.append(
            jnp.where(
                iota((1, T), 1) + base >= start_last, jnp.exp(gcol[T - 1 : T, :] - grow), 0.0
            )
        )
        d_last.append(into[T - 1 : T, :])
    same_sub = (row >> 4) == (lane >> 4)
    for j in range(SUB - 1):
        pick[:, j * T : (j + 1) * T] = (same_sub & ((row & 15) == j)).astype(F32).astype(BF)

    nxt = (lax.rem(c + 1, NX * NZ), hd)
    sends = []

    def send(i, src, dst, recv, dev):
        cp = pltpu.make_async_remote_copy(
            src_ref=src, dst_ref=dst, send_sem=ss.at[i], recv_sem=recv,
            device_id=dev, device_id_type=MESH,
        )
        cp.start()
        sends.append(cp)
        return cp

    l_tok.wait()
    l_wk.wait()
    pk[...] = mm(tok[...], wk[...]).astype(BF)
    pl.semaphore_wait(barrier, len(sources))
    c_hk = send(0, pk.at[T - 16 : T], hk, rs_halo.at[0], nxt)
    l_wq.wait()
    pq[...] = mm(tok[...], wq[...]).astype(BF)
    c_hq = send(1, pq.at[T - 16 : T], hq, rs_halo.at[1], nxt)
    l_wv.wait()
    pv[...] = mm(tok[...], wv[...]).astype(BF)
    c_hv = send(2, pv.at[T - 16 : T], hv, rs_halo.at[2], nxt)
    l_wg.wait()
    gate = mm(tok[...], wg[...]).astype(BF).astype(F32)
    sg[...] = gate / (1.0 + jnp.exp(-gate))

    ext[8 : 8 + T, 0:256] = pk[...].astype(F32)
    ext[8 : 8 + T, 256:512] = pq[...].astype(F32)
    ext[8 : 8 + T, 512:1024] = pv[...].astype(F32)
    l_ck.wait()
    l_cq.wait()
    l_cv.wait()
    c_hk.wait_recv()
    c_hq.wait_recv()
    c_hv.wait_recv()
    ext[0:8, 0:256] = hk[...].astype(F32)[8:16]
    ext[0:8, 256:512] = hq[...].astype(F32)[8:16]
    ext[0:8, 512:1024] = hv[...].astype(F32)[8:16]

    def conv(first, taps, col):
        wide = slice(first + col, first + col + W)
        w = taps[...].astype(F32)[:, col : col + W]
        acc = w[3:4] * ext[8 : 8 + T, wide]
        for s in (1, 2, 3):
            acc = acc + jnp.where(age >= s, w[3 - s : 4 - s] * ext[8 - s : 8 - s + T, wide], 0.0)
        return acc / (1.0 + jnp.exp(-acc))

    def unit(a):
        return a * lax.rsqrt(jnp.sum(a * a, axis=-1, keepdims=True) + 1e-6)

    keys = [unit(conv(0, ck, n * W)) for n in range(HK)]
    queries = [unit(conv(256, cq, n * W)) * W ** -0.5 for n in range(HK)]
    grams, scores, keys_t = [], [], []
    for n in range(HK):
        kb = keys[n].astype(BF)
        r = mm_t(jnp.concatenate([kb, queries[n].astype(BF)], axis=0), kb)
        grams.append(r[:T])
        scores.append(r[T:])
        keys_t.append(jnp.transpose(keys[n]))
    values = [conv(512, cv, h * W) for h in range(HV)]

    low = [bdm[h] * grams[h // 2] for h in range(HV)]
    packed = []
    lane16 = iota((SUB, T), 1)
    for h in range(HV):
        p = None
        for b in range(T // SUB):
            q = jnp.where((lane16 >> 4) == b, low[h][b * SUB : (b + 1) * SUB], 0.0)
            p = q if p is None else p + q
        packed.append(p)
    coef = mm(jnp.concatenate(packed, axis=0).astype(BF), pick[...])
    inv = [(iota((SUB, T), 0) == (lane16 & 15)).astype(F32) for _ in range(HV)]
    for j in range(SUB - 1):
        for h in range(HV):
            cj = coef[h * SUB : (h + 1) * SUB, j * T : (j + 1) * T]
            inv[h] = inv[h] - cj * inv[h][j : j + 1, :]
    full = [jnp.where(same_sub, jnp.concatenate([inv[h]] * (T // SUB), axis=0), 0.0) for h in range(HV)]
    for shift in (4, 5, 6):
        cut = ((row >> (shift + 1)) == (lane >> (shift + 1))) & ((row >> shift) != (lane >> shift)) & strict
        fb = [full[h].astype(BF) for h in range(HV)]
        m1 = [mm(jnp.where(cut, low[h], 0.0).astype(BF), fb[h]).astype(BF) for h in range(HV)]
        full = [full[h] - mm(fb[h], m1[h]) for h in range(HV)]

    uw = []
    for h in range(HV):
        beta = bcol[h]
        right = jnp.concatenate(
            [(beta * values[h]).astype(BF), (beta * dcol[h] * keys[h // 2]).astype(BF)], axis=1
        )
        uw.append(mm(full[h].astype(BF), right).astype(BF))
    eye = (row == lane).astype(F32)
    for h in range(HV):
        mu = mm((keys_t[h // 2] * f_row[h]).astype(BF), uw[h])
        psend[h] = jnp.concatenate([eye * d_last[h] - mu[:, W:], mu[:, :W]], axis=1).astype(BF)

    c_x = [
        send(2 + d, psend.at[lax.rem(x + d, NX)], pbuf.at[1, x], rs_x.at[d - 1], at_zx(0, d))
        for d in (1, 2, 3)
    ]
    c_z = [
        send(6 + d, psend.at[lax.rem(x + d, NX)], pbuf.at[0, x], rs_z.at[d], at_zx(1, d))
        for d in range(NX)
    ]
    pbuf[1, x] = psend[x]

    for h in range(HV):
        n = h // 2
        oq = mm((dm[h] * scores[n]).astype(BF), uw[h])
        o1[h] = oq[:, :W]
        qt[h] = (dcol[h] * queries[n] - oq[:, W:]).astype(BF)

    for cp in c_x:
        cp.wait_recv()

    def joined(later, earlier):
        r = mm(later[:, :W], earlier)
        return jnp.concatenate([r[:, :W], r[:, W:] + later[:, W:].astype(F32)], axis=1).astype(BF)

    own = [pbuf[1, b] for b in range(NX)]
    c10 = joined(own[1], own[0])
    c32 = joined(own[3], own[2])
    c210 = joined(own[2], c10)
    c3210 = joined(c32, c10)
    for cp in c_z:
        cp.wait_recv()
    prv = [pbuf[0, b] for b in range(NX)]
    p10 = joined(prv[1], prv[0])
    p32 = joined(prv[3], prv[2])
    p3210 = joined(p32, p10)
    two = joined(c3210, p3210)
    qs[0] = two[:, :W]
    qs[1] = two[:, W:]
    c_b1 = send(10, qs, rb_mu, rs_b.at[0], at_zx(1, 0))
    c_b3 = send(11, qs.at[1], rb_u, rs_b.at[1], at_zx(3, 0))
    c_b1.wait_recv()
    c_b3.wait_recv()
    enter = (mm(rb_mu[0], rb_u[...]) + rb_mu[1].astype(F32)).astype(BF)
    ssend[0] = enter
    for b, pair in ((1, own[0]), (2, c10), (3, c210)):
        ssend[b] = (mm(pair[:, :W], enter) + pair[:, W:].astype(F32)).astype(BF)
    c_r = [
        send(11 + d, ssend.at[lax.rem(x + d, NX)], srecv.at[x], rs_r.at[d - 1], at_zx(0, d))
        for d in (1, 2, 3)
    ]
    srecv[x] = ssend[x]
    for cp in c_r:
        cp.wait_recv()

    for h in range(HV):
        o = o1[h] + mm(qt[h], srecv[h])
        o = o * lax.rsqrt(jnp.mean(o * o, axis=-1, keepdims=True) + 1e-6)
        yb[:, h * W : (h + 1) * W] = (o * sg[:, h * W : (h + 1) * W]).astype(BF)
    l_wo.wait()
    cw = D // NCH
    c_c = []
    for n in range(NCH):
        part = mm(yb[...], wo[:, n * cw : (n + 1) * cw]).astype(BF)
        for k in range(2 * NY):
            pm[n, k % 2, k // 2] = part[k * 16 : (k + 1) * 16]
        c_c.append(send(15 + n, pm.at[n, 1 - co], rc.at[n], rs_c.at[n], partner))
    c_y = []
    for n in range(NCH):
        c_c[n].wait_recv()
        s2[n] = (pm[n, co].astype(F32) + rc[n].astype(F32)).astype(BF)
        c_y.append([
            send(15 + NCH + 3 * n + d - 1, s2.at[n, lax.rem(y + d, NY)], ry.at[n, d - 1], rs_y.at[n, d - 1], at_y(d))
            for d in (1, 2, 3)
        ])
    for n in range(NCH):
        for cp in c_y[n]:
            cp.wait_recv()
        tot = pm[n, co, y].astype(F32) + rc[n, y].astype(F32)
        for d in range(3):
            tot = tot + ry[n, d].astype(F32)
        out_ref[:, n * cw : (n + 1) * cw] = tot.astype(BF)
    for cp in sends:
        cp.wait_send()


def per_device(*args):
    vm = pltpu.VMEM
    dma = pltpu.SemaphoreType.DMA
    any_spec = pl.BlockSpec(memory_space=pl.ANY)
    return pl.pallas_call(
        kernel,
        out_shape=jax.ShapeDtypeStruct((16, D), BF),
        in_specs=[any_spec] * 13,
        out_specs=pl.BlockSpec(memory_space=pltpu.VMEM),
        scratch_shapes=[
            vm((T, D), BF), vm((D, 256), BF), vm((D, 256), BF), vm((D, 512), BF), vm((D, 512), BF),
            vm((512, D), BF), vm((4, 256), BF), vm((4, 256), BF), vm((4, 512), BF),
            vm((HV, T), F32), vm((HV, T), F32), pltpu.SMEM((DOCS,), jnp.int32), pltpu.SMEM((HV,), F32),
            vm((T, 256), BF), vm((T, 256), BF), vm((T, 512), BF),
            vm((16, 256), BF), vm((16, 256), BF), vm((16, 512), BF),
            vm((T + 8, 1024), F32), vm((2 * HV, T), F32),
            vm((HV, T, T), F32), vm((HV, T, T), F32), vm((HV, T, T), F32), vm((HV, T, T), F32),
            vm((T, (SUB - 1) * T), BF),
            vm((T, 512), F32),
            vm((HV, W, 2 * W), BF), vm((2, NX, W, 2 * W), BF),
            vm((HV, T, W), F32), vm((HV, T, W), BF),
            vm((2, W, W), BF), vm((2, W, W), BF), vm((W, W), BF),
            vm((NX, W, W), BF), vm((HV, W, W), BF),
            vm((T, 512), BF),
            vm((NCH, 2, NY, 16, D // NCH), BF), vm((NCH, NY, 16, D // NCH), BF),
            vm((NCH, NY, 16, D // NCH), BF), vm((NCH, 3, 16, D // NCH), BF),
            dma((13,)), dma((15 + NCH * 4,)), dma((3,)), dma((3,)), dma((4,)), dma((2,)), dma((3,)),
            dma((NCH,)), dma((NCH, 3)),
        ],
        name="layer",
        compiler_params=pltpu.CompilerParams(
            collective_id=0, has_side_effects=True, vmem_limit_bytes=56 << 20
        ),
    )(*args)


def solution(mesh):
    in_specs = (
        P("ctx", None),
        P(),
        P(None, "head"),
        P(None, "head"),
        P(None, "head"),
        P(None, "head"),
        P(None, "head"),
        P(None, "head"),
        P(None, "head"),
        P("head", "ctx"),
        P("head", "ctx"),
        P("head"),
        P("head", None),
    )
    out_specs = P(("ctx", "head"), None)
    return jax.shard_map(
        per_device, mesh=mesh, in_specs=in_specs, out_specs=out_specs, check_vma=False
    )
```

```python
import jax
import jax.numpy as jnp
from jax import lax
from jax.experimental import pallas as pl
from jax.experimental.pallas import tpu as pltpu
from jax.sharding import PartitionSpec as P

MESH = pl.DeviceIdType.MESH
F32 = jnp.float32
BF = jnp.bfloat16
T = 128
W = 128
NX = 4
NZ = 8
NY = 4
HV = 4
HK = 2
DOCS = 16
SUB = 16
NCH = 1
D = 2048


def mm(a, b):
    return jnp.dot(a, b, preferred_element_type=F32)


def mm_t(a, b):
    return lax.dot_general(a, b, (((1,), (1,)), ((), ())), preferred_element_type=F32)


def iota(shape, dim):
    return lax.broadcasted_iota(jnp.int32, shape, dim)


def kernel(
    tok_h, doc_h, wq_h, wk_h, wv_h, wg_h, cq_h, ck_h, cv_h, bl_h, dl_h, al_h, wo_h,
    out_ref,
    tok, wq, wk, wv, wg, wo, cq, ck, cv, bl, dl, doc_s, al_s,
    pk, pq, pv, hk, hq, hv, ext, sc8, dm, bdm, dcol, bcol, pick,
    sg, psend, pbuf, o1, qt, qs, rb_mu, rb_u, ssend, srecv, yb, pm, rc, s2, ry,
    lsem, ss, rs_halo, rs_x, rs_z, rs_b, rs_r, rs_c, rs_y,
):
    c = lax.axis_index("ctx")
    hd = lax.axis_index("head")
    z, x = c // NX, c % NX
    y, co = hd // 2, hd % 2

    def at_zx(dz, dx):
        return (lax.rem(z + dz + NZ, NZ) * NX + lax.rem(x + dx, NX), hd)

    def at_y(dy):
        return (c, lax.rem(y + dy, NY) * 2 + co)

    partner = (c, y * 2 + 1 - co)

    def load(i, src, dst):
        cp = pltpu.make_async_copy(src, dst, lsem.at[i])
        cp.start()
        return cp

    l_doc = load(0, doc_h, doc_s)
    l_al = load(1, al_h, al_s)
    l_bl = load(2, bl_h, bl)
    l_dl = load(3, dl_h, dl)
    l_tok = load(4, tok_h, tok)
    l_wk = load(5, wk_h, wk)
    l_wv = load(7, wv_h, wv)

    barrier = pltpu.get_barrier_semaphore()
    sources = [at_zx(0, d) for d in (1, 2, 3)]
    sources += [at_zx(-1, d) for d in range(NX)]
    sources += [at_zx(-3, 0), partner]
    sources += [at_y(d) for d in (1, 2, 3)]
    for dev in sources:
        pl.semaphore_signal(barrier, inc=1, device_id=dev, device_id_type=MESH)

    l_ck = load(8, ck_h, ck)
    l_cv = load(10, cv_h, cv)
    l_wq = load(6, wq_h, wq)
    l_cq = load(9, cq_h, cq)
    l_wg = load(11, wg_h, wg)
    l_wo = load(12, wo_h, wo)

    l_doc.wait()
    l_al.wait()
    l_bl.wait()
    l_dl.wait()
    base = c * T
    offs = []
    total = jnp.int32(0)
    for j in range(DOCS):
        offs.append(total)
        total = total + doc_s[j]
    row = iota((T, T), 0)
    lane = iota((T, T), 1)
    start = jnp.zeros((T, T), jnp.int32)
    start_last = jnp.int32(0)
    for j in range(1, DOCS):
        start = jnp.where(offs[j] <= row + base, offs[j], start)
        start_last = jnp.where(offs[j] <= base + T - 1, offs[j], start_last)
    age = row + base - start
    kept = start < base
    lower = (lane <= row) & (base + lane >= start)
    strict = lane < row
    dlv = dl[...]
    soft = jnp.maximum(dlv, 0.0) + jnp.log(1.0 + jnp.exp(-jnp.abs(dlv)))
    r4 = iota((HV, T), 0)
    rate = jnp.where(r4 == 0, al_s[0], jnp.where(r4 == 1, al_s[1], jnp.where(r4 == 2, al_s[2], al_s[3])))
    sc8[0:HV] = -jnp.exp(rate) * soft
    sc8[HV : 2 * HV] = 1.0 / (1.0 + jnp.exp(-bl[...]))
    both = sc8[...]
    upper = (row <= lane).astype(F32)
    cum = jnp.dot(both, upper, preferred_element_type=F32, precision=lax.Precision.HIGHEST)
    both = jnp.where(iota((2 * HV, T), 0) < HV, cum, both)
    cols = jnp.transpose(both)
    f_row, d_last = [], []
    for h in range(HV):
        gcol = jnp.broadcast_to(cols[:, h : h + 1], (T, T))
        grow = both[h : h + 1, :]
        decay = jnp.exp(jnp.where(lower, gcol - grow, -1e30))
        beta = jnp.broadcast_to(cols[:, HV + h : HV + h + 1], (T, T))
        into = jnp.where(kept, jnp.exp(gcol), 0.0)
        dm[h] = decay
        bdm[h] = jnp.where(strict, decay * beta, 0.0)
        dcol[h] = into
        bcol[h] = beta
        f_row.append(
            jnp.where(
                iota((1, T), 1) + base >= start_last, jnp.exp(gcol[T - 1 : T, :] - grow), 0.0
            )
        )
        d_last.append(into[T - 1 : T, :])
    same_sub = (row >> 4) == (lane >> 4)
    for j in range(SUB - 1):
        pick[:, j * T : (j + 1) * T] = (same_sub & ((row & 15) == j)).astype(F32).astype(BF)

    nxt = (lax.rem(c + 1, NX * NZ), hd)
    sends = []

    def send(i, src, dst, recv, dev):
        cp = pltpu.make_async_remote_copy(
            src_ref=src, dst_ref=dst, send_sem=ss.at[i], recv_sem=recv,
            device_id=dev, device_id_type=MESH,
        )
        cp.start()
        sends.append(cp)
        return cp

    l_tok.wait()
    l_wk.wait()
    pk[...] = mm(tok[...], wk[...]).astype(BF)
    pl.semaphore_wait(barrier, len(sources))
    c_hk = send(0, pk.at[T - 16 : T], hk, rs_halo.at[0], nxt)
    l_wv.wait()
    pv[...] = mm(tok[...], wv[...]).astype(BF)
    c_hv = send(2, pv.at[T - 16 : T], hv, rs_halo.at[2], nxt)
    l_wq.wait()
    pq[...] = mm(tok[...], wq[...]).astype(BF)
    c_hq = send(1, pq.at[T - 16 : T], hq, rs_halo.at[1], nxt)
    l_wg.wait()
    sg[...] = mm(tok[...], wg[...]).astype(BF).astype(F32)

    ext[8 : 8 + T, 0:256] = pk[...].astype(F32)
    ext[8 : 8 + T, 256:512] = pq[...].astype(F32)
    ext[8 : 8 + T, 512:1024] = pv[...].astype(F32)
    l_ck.wait()
    l_cv.wait()
    l_cq.wait()

    def conv(first, taps, col):
        wide = slice(first + col, first + col + W)
        w = taps[...].astype(F32)[:, col : col + W]
        acc = w[3:4] * ext[8 : 8 + T, wide]
        for s in (1, 2, 3):
            acc = acc + jnp.where(age >= s, w[3 - s : 4 - s] * ext[8 - s : 8 - s + T, wide], 0.0)
        return acc / (1.0 + jnp.exp(-acc))

    def unit(a):
        return a * lax.rsqrt(jnp.sum(a * a, axis=-1, keepdims=True) + 1e-6)

    c_hk.wait_recv()
    ext[0:8, 0:256] = hk[...].astype(F32)[8:16]
    keys = [unit(conv(0, ck, n * W)) for n in range(HK)]
    keys_b = [k.astype(BF) for k in keys]
    keys_t = [jnp.transpose(k) for k in keys]
    grams = [mm_t(k, k) for k in keys_b]
    c_hv.wait_recv()
    ext[0:8, 512:1024] = hv[...].astype(F32)[8:16]
    values = [conv(512, cv, h * W) for h in range(HV)]

    low = [bdm[h] * grams[h // 2] for h in range(HV)]
    packed = []
    lane16 = iota((SUB, T), 1)
    for h in range(HV):
        p = None
        for b in range(T // SUB):
            q = jnp.where((lane16 >> 4) == b, low[h][b * SUB : (b + 1) * SUB], 0.0)
            p = q if p is None else p + q
        packed.append(p)
    coef = mm(jnp.concatenate(packed, axis=0).astype(BF), pick[...])
    inv = [(iota((SUB, T), 0) == (lane16 & 15)).astype(F32) for _ in range(HV)]
    for j in range(SUB - 1):
        for h in range(HV):
            cj = coef[h * SUB : (h + 1) * SUB, j * T : (j + 1) * T]
            inv[h] = inv[h] - cj * inv[h][j : j + 1, :]
    full = [jnp.where(same_sub, jnp.concatenate([inv[h]] * (T // SUB), axis=0), 0.0) for h in range(HV)]
    for shift in (4, 5, 6):
        cut = ((row >> (shift + 1)) == (lane >> (shift + 1))) & ((row >> shift) != (lane >> shift)) & strict
        fb = [full[h].astype(BF) for h in range(HV)]
        m1 = [mm(jnp.where(cut, low[h], 0.0).astype(BF), fb[h]).astype(BF) for h in range(HV)]
        full = [full[h] - mm(fb[h], m1[h]) for h in range(HV)]

    uw = []
    for h in range(HV):
        beta = bcol[h]
        right = jnp.concatenate(
            [(beta * values[h]).astype(BF), (beta * dcol[h] * keys[h // 2]).astype(BF)], axis=1
        )
        uw.append(mm(full[h].astype(BF), right).astype(BF))
    eye = (row == lane).astype(F32)
    for h in range(HV):
        mu = mm((keys_t[h // 2] * f_row[h]).astype(BF), uw[h])
        psend[h] = jnp.concatenate([eye * d_last[h] - mu[:, W:], mu[:, :W]], axis=1).astype(BF)

    c_z = [
        send(6 + d, psend.at[lax.rem(x + d, NX)], pbuf.at[0, x], rs_z.at[d], at_zx(1, d))
        for d in range(NX)
    ]
    c_x = [
        send(2 + d, psend.at[lax.rem(x + d, NX)], pbuf.at[1, x], rs_x.at[d - 1], at_zx(0, d))
        for d in (1, 2, 3)
    ]
    pbuf[1, x] = psend[x]

    c_hq.wait_recv()
    ext[0:8, 256:512] = hq[...].astype(F32)[8:16]
    queries = [unit(conv(256, cq, n * W)) * W ** -0.5 for n in range(HK)]
    scores = [mm_t(queries[n].astype(BF), keys_b[n]) for n in range(HK)]
    gate = sg[...]
    sg[...] = gate / (1.0 + jnp.exp(-gate))
    for h in range(HV):
        n = h // 2
        oq = mm((dm[h] * scores[n]).astype(BF), uw[h])
        o1[h] = oq[:, :W]
        qt[h] = (dcol[h] * queries[n] - oq[:, W:]).astype(BF)

    for cp in c_x:
        cp.wait_recv()

    def joined(later, earlier):
        r = mm(later[:, :W], earlier)
        return jnp.concatenate([r[:, :W], r[:, W:] + later[:, W:].astype(F32)], axis=1).astype(BF)

    own = [pbuf[1, b] for b in range(NX)]
    c10 = joined(own[1], own[0])
    c32 = joined(own[3], own[2])
    c210 = joined(own[2], c10)
    c3210 = joined(c32, c10)
    for cp in c_z:
        cp.wait_recv()
    prv = [pbuf[0, b] for b in range(NX)]
    p10 = joined(prv[1], prv[0])
    p32 = joined(prv[3], prv[2])
    p3210 = joined(p32, p10)
    two = joined(c3210, p3210)
    qs[0] = two[:, :W]
    qs[1] = two[:, W:]
    c_b3 = send(11, qs.at[1], rb_u, rs_b.at[1], at_zx(3, 0))
    c_b1 = send(10, qs, rb_mu, rs_b.at[0], at_zx(1, 0))
    c_b1.wait_recv()
    c_b3.wait_recv()
    enter = (mm(rb_mu[0], rb_u[...]) + rb_mu[1].astype(F32)).astype(BF)
    ssend[0] = enter
    for b, pair in ((1, own[0]), (2, c10), (3, c210)):
        ssend[b] = (mm(pair[:, :W], enter) + pair[:, W:].astype(F32)).astype(BF)
    c_r = [
        send(11 + d, ssend.at[lax.rem(x + d, NX)], srecv.at[x], rs_r.at[d - 1], at_zx(0, d))
        for d in (1, 2, 3)
    ]
    srecv[x] = ssend[x]
    for cp in c_r:
        cp.wait_recv()

    for h in range(HV):
        o = o1[h] + mm(qt[h], srecv[h])
        o = o * lax.rsqrt(jnp.mean(o * o, axis=-1, keepdims=True) + 1e-6)
        yb[:, h * W : (h + 1) * W] = (o * sg[:, h * W : (h + 1) * W]).astype(BF)
    l_wo.wait()
    cw = D // NCH
    c_c = []
    for n in range(NCH):
        part = mm(yb[...], wo[:, n * cw : (n + 1) * cw]).astype(BF)
        for k in range(2 * NY):
            pm[n, k % 2, k // 2] = part[k * 16 : (k + 1) * 16]
        c_c.append(send(15 + n, pm.at[n, 1 - co], rc.at[n], rs_c.at[n], partner))
    c_y = []
    for n in range(NCH):
        c_c[n].wait_recv()
        s2[n] = (pm[n, co].astype(F32) + rc[n].astype(F32)).astype(BF)
        c_y.append([
            send(15 + NCH + 3 * n + d - 1, s2.at[n, lax.rem(y + d, NY)], ry.at[n, d - 1], rs_y.at[n, d - 1], at_y(d))
            for d in (1, 2, 3)
        ])
    for n in range(NCH):
        for cp in c_y[n]:
            cp.wait_recv()
        tot = pm[n, co, y].astype(F32) + rc[n, y].astype(F32)
        for d in range(3):
            tot = tot + ry[n, d].astype(F32)
        out_ref[:, n * cw : (n + 1) * cw] = tot.astype(BF)
    for cp in sends:
        cp.wait_send()


def per_device(*args):
    vm = pltpu.VMEM
    dma = pltpu.SemaphoreType.DMA
    any_spec = pl.BlockSpec(memory_space=pl.ANY)
    return pl.pallas_call(
        kernel,
        out_shape=pltpu.VMEM((16, D), BF),
        in_specs=[any_spec] * 13,
        out_specs=pl.BlockSpec(memory_space=pltpu.VMEM),
        scratch_shapes=[
            vm((T, D), BF), vm((D, 256), BF), vm((D, 256), BF), vm((D, 512), BF), vm((D, 512), BF),
            vm((512, D), BF), vm((4, 256), BF), vm((4, 256), BF), vm((4, 512), BF),
            vm((HV, T), F32), vm((HV, T), F32), pltpu.SMEM((DOCS,), jnp.int32), pltpu.SMEM((HV,), F32),
            vm((T, 256), BF), vm((T, 256), BF), vm((T, 512), BF),
            vm((16, 256), BF), vm((16, 256), BF), vm((16, 512), BF),
            vm((T + 8, 1024), F32), vm((2 * HV, T), F32),
            vm((HV, T, T), F32), vm((HV, T, T), F32), vm((HV, T, T), F32), vm((HV, T, T), F32),
            vm((T, (SUB - 1) * T), BF),
            vm((T, 512), F32),
            vm((HV, W, 2 * W), BF), vm((2, NX, W, 2 * W), BF),
            vm((HV, T, W), F32), vm((HV, T, W), BF),
            vm((2, W, W), BF), vm((2, W, W), BF), vm((W, W), BF),
            vm((NX, W, W), BF), vm((HV, W, W), BF),
            vm((T, 512), BF),
            vm((NCH, 2, NY, 16, D // NCH), BF), vm((NCH, NY, 16, D // NCH), BF),
            vm((NCH, NY, 16, D // NCH), BF), vm((NCH, 3, 16, D // NCH), BF),
            dma((13,)), dma((15 + NCH * 4,)), dma((3,)), dma((3,)), dma((4,)), dma((2,)), dma((3,)),
            dma((NCH,)), dma((NCH, 3)),
        ],
        name="layer",
        compiler_params=pltpu.CompilerParams(
            collective_id=0, has_side_effects=True, vmem_limit_bytes=56 << 20
        ),
    )(*args)


def solution(mesh):
    in_specs = (
        P("ctx", None),
        P(),
        P(None, "head"),
        P(None, "head"),
        P(None, "head"),
        P(None, "head"),
        P(None, "head"),
        P(None, "head"),
        P(None, "head"),
        P("head", "ctx"),
        P("head", "ctx"),
        P("head"),
        P("head", None),
    )
    out_specs = P(("ctx", "head"), None)
    return jax.shard_map(
        per_device, mesh=mesh, in_specs=in_specs, out_specs=out_specs, check_vma=False
    )
```

```python
import jax
import jax.numpy as jnp
from jax import lax
from jax.experimental import pallas as pl
from jax.experimental.pallas import tpu as pltpu
from jax.sharding import PartitionSpec as P

MESH = pl.DeviceIdType.MESH
F32 = jnp.float32
BF = jnp.bfloat16
T = 128
W = 128
NX = 4
NZ = 8
NY = 4
HV = 4
HK = 2
DOCS = 16
SUB = 16
NCH = 1
D = 2048


def mm(a, b):
    return jnp.dot(a, b, preferred_element_type=F32)


def mm_t(a, b):
    return lax.dot_general(a, b, (((1,), (1,)), ((), ())), preferred_element_type=F32)


def iota(shape, dim):
    return lax.broadcasted_iota(jnp.int32, shape, dim)


def kernel(
    tok_h, doc_h, wq_h, wk_h, wv_h, wg_h, cq_h, ck_h, cv_h, bl_h, dl_h, al_h, wo_h,
    out_ref,
    tok, wq, wk, wv, wg, wo, cq, ck, cv, bl, dl, doc_s, al_s,
    pk, pq, pv, hk, hq, hv, ext, sc8, dm, bdm, dcol, bcol, pick,
    sg, psend, pbuf, o1, qt, qs, rb_mu, rb_u, ssend, srecv, yb, pm, rc, s2, ry,
    ready_h, ready_1, ready_3, lsem, ss, rs_halo, rs_x, rs_z, rs_b, rs_r, rs_c, rs_y,
):
    c = lax.axis_index("ctx")
    hd = lax.axis_index("head")
    z, x = c // NX, c % NX
    y, co = hd // 2, hd % 2

    def at_zx(dz, dx):
        return (lax.rem(z + dz + NZ, NZ) * NX + lax.rem(x + dx, NX), hd)

    def at_y(dy):
        return (c, lax.rem(y + dy, NY) * 2 + co)

    partner = (c, y * 2 + 1 - co)

    def load(i, src, dst):
        cp = pltpu.make_async_copy(src, dst, lsem.at[i])
        cp.start()
        return cp

    l_doc = load(0, doc_h, doc_s)
    l_al = load(1, al_h, al_s)
    l_bl = load(2, bl_h, bl)
    l_dl = load(3, dl_h, dl)
    l_tok = load(4, tok_h, tok)
    l_wk = load(5, wk_h, wk)
    l_wv = load(7, wv_h, wv)

    barrier = pltpu.get_barrier_semaphore()

    def hello(sem, dev):
        pl.semaphore_signal(sem, inc=1, device_id=dev, device_id_type=MESH)

    mates = [at_zx(0, d) for d in (1, 2, 3)] + [partner] + [at_y(d) for d in (1, 2, 3)]
    for dev in mates:
        hello(barrier, dev)

    @pl.when(z < NZ - 1)
    def _():
        for d in range(NX):
            hello(barrier, at_zx(1, d))

    @pl.when(z < NZ - 3)
    def _():
        hello(barrier, at_zx(3, 0))

    l_ck = load(8, ck_h, ck)
    l_cv = load(10, cv_h, cv)
    l_wq = load(6, wq_h, wq)
    l_cq = load(9, cq_h, cq)
    l_wg = load(11, wg_h, wg)
    l_wo = load(12, wo_h, wo)

    l_doc.wait()
    l_al.wait()
    l_bl.wait()
    l_dl.wait()
    base = c * T
    offs = []
    total = jnp.int32(0)
    for j in range(DOCS):
        offs.append(total)
        total = total + doc_s[j]
    row = iota((T, T), 0)
    lane = iota((T, T), 1)
    start = jnp.zeros((T, T), jnp.int32)
    start_last = jnp.int32(0)
    for j in range(1, DOCS):
        start = jnp.where(offs[j] <= row + base, offs[j], start)
        start_last = jnp.where(offs[j] <= base + T - 1, offs[j], start_last)
    age = row + base - start
    kept = start < base
    lower = (lane <= row) & (base + lane >= start)
    strict = lane < row
    dlv = dl[...]
    soft = jnp.maximum(dlv, 0.0) + jnp.log(1.0 + jnp.exp(-jnp.abs(dlv)))
    r4 = iota((HV, T), 0)
    rate = jnp.where(r4 == 0, al_s[0], jnp.where(r4 == 1, al_s[1], jnp.where(r4 == 2, al_s[2], al_s[3])))
    sc8[0:HV] = -jnp.exp(rate) * soft
    sc8[HV : 2 * HV] = 1.0 / (1.0 + jnp.exp(-bl[...]))
    both = sc8[...]
    upper = (row <= lane).astype(F32)
    cum = jnp.dot(both, upper, preferred_element_type=F32, precision=lax.Precision.HIGHEST)
    both = jnp.where(iota((2 * HV, T), 0) < HV, cum, both)
    cols = jnp.transpose(both)
    f_row, d_last = [], []
    for h in range(HV):
        gcol = jnp.broadcast_to(cols[:, h : h + 1], (T, T))
        grow = both[h : h + 1, :]
        decay = jnp.exp(jnp.where(lower, gcol - grow, -1e30))
        beta = jnp.broadcast_to(cols[:, HV + h : HV + h + 1], (T, T))
        into = jnp.where(kept, jnp.exp(gcol), 0.0)
        dm[h] = decay
        bdm[h] = jnp.where(strict, decay * beta, 0.0)
        dcol[h] = into
        bcol[h] = beta
        f_row.append(
            jnp.where(
                iota((1, T), 1) + base >= start_last, jnp.exp(gcol[T - 1 : T, :] - grow), 0.0
            )
        )
        d_last.append(into[T - 1 : T, :])
    same_sub = (row >> 4) == (lane >> 4)
    for j in range(SUB - 1):
        pick[:, j * T : (j + 1) * T] = (same_sub & ((row & 15) == j)).astype(F32).astype(BF)

    @pl.when(c == 0)
    def _():
        hk[...] = jnp.zeros_like(hk)
        hq[...] = jnp.zeros_like(hq)
        hv[...] = jnp.zeros_like(hv)

    @pl.when(z == 0)
    def _():
        pbuf[0] = jnp.zeros((NX, W, 2 * W), BF)
        rb_mu[...] = jnp.zeros_like(rb_mu)

    @pl.when(z < 3)
    def _():
        rb_u[...] = jnp.zeros_like(rb_u)

    earlier = jnp.where(z > 0, NX, 0) + jnp.where(z > 2, 1, 0)
    pl.semaphore_wait(barrier, len(mates) + earlier)

    @pl.when(z > 0)
    def _():
        for d in range(NX):
            hello(ready_1.at[(NX - d) % NX], at_zx(-1, d))

    @pl.when((z > 0) & (x == 0))
    def _():
        hello(ready_h, at_zx(-1, NX - 1))

    @pl.when(z > 2)
    def _():
        hello(ready_3, at_zx(-3, 0))

    nxt = (lax.rem(c + 1, NX * NZ), hd)
    sends = []

    def copy(i, src, dst, recv, dev):
        return pltpu.make_async_remote_copy(
            src_ref=src, dst_ref=dst, send_sem=ss.at[i], recv_sem=recv,
            device_id=dev, device_id_type=MESH,
        )

    def send(i, src, dst, recv, dev):
        cp = copy(i, src, dst, recv, dev)
        cp.start()
        sends.append((None, cp))
        return cp

    def send_if(cond, cp):
        @pl.when(cond)
        def _():
            cp.start()

    c_hk = copy(0, pk.at[T - 16 : T], hk, rs_halo.at[0], nxt)
    c_hq = copy(1, pq.at[T - 16 : T], hq, rs_halo.at[1], nxt)
    c_hv = copy(2, pv.at[T - 16 : T], hv, rs_halo.at[2], nxt)
    sends += [(c < NX * NZ - 1, cp) for cp in (c_hk, c_hq, c_hv)]
    inner = x < NX - 1
    l_tok.wait()
    l_wk.wait()
    pk[...] = mm(tok[...], wk[...]).astype(BF)
    send_if(inner, c_hk)
    l_wv.wait()
    pv[...] = mm(tok[...], wv[...]).astype(BF)
    send_if(inner, c_hv)
    l_wq.wait()
    pq[...] = mm(tok[...], wq[...]).astype(BF)
    send_if(inner, c_hq)

    @pl.when((x == NX - 1) & (z < NZ - 1))
    def _():
        pl.semaphore_wait(ready_h, 1)
        c_hk.start()
        c_hv.start()
        c_hq.start()

    l_wg.wait()
    sg[...] = mm(tok[...], wg[...]).astype(BF).astype(F32)

    ext[8 : 8 + T, 0:256] = pk[...].astype(F32)
    ext[8 : 8 + T, 256:512] = pq[...].astype(F32)
    ext[8 : 8 + T, 512:1024] = pv[...].astype(F32)
    l_ck.wait()
    l_cv.wait()
    l_cq.wait()

    def conv(first, taps, col):
        wide = slice(first + col, first + col + W)
        w = taps[...].astype(F32)[:, col : col + W]
        acc = w[3:4] * ext[8 : 8 + T, wide]
        for s in (1, 2, 3):
            acc = acc + jnp.where(age >= s, w[3 - s : 4 - s] * ext[8 - s : 8 - s + T, wide], 0.0)
        return acc / (1.0 + jnp.exp(-acc))

    def unit(a):
        return a * lax.rsqrt(jnp.sum(a * a, axis=-1, keepdims=True) + 1e-6)


    @pl.when(c > 0)
    def _():
        c_hk.wait_recv()

    ext[0:8, 0:256] = hk[...].astype(F32)[8:16]
    keys = [unit(conv(0, ck, n * W)) for n in range(HK)]
    keys_b = [k.astype(BF) for k in keys]
    keys_t = [jnp.transpose(k) for k in keys]
    grams = [mm_t(k, k) for k in keys_b]

    @pl.when(c > 0)
    def _():
        c_hv.wait_recv()

    ext[0:8, 512:1024] = hv[...].astype(F32)[8:16]
    values = [conv(512, cv, h * W) for h in range(HV)]

    low = [bdm[h] * grams[h // 2] for h in range(HV)]
    packed = []
    lane16 = iota((SUB, T), 1)
    for h in range(HV):
        p = None
        for b in range(T // SUB):
            q = jnp.where((lane16 >> 4) == b, low[h][b * SUB : (b + 1) * SUB], 0.0)
            p = q if p is None else p + q
        packed.append(p)
    coef = mm(jnp.concatenate(packed, axis=0).astype(BF), pick[...])
    inv = [(iota((SUB, T), 0) == (lane16 & 15)).astype(F32) for _ in range(HV)]
    for j in range(SUB - 1):
        for h in range(HV):
            cj = coef[h * SUB : (h + 1) * SUB, j * T : (j + 1) * T]
            inv[h] = inv[h] - cj * inv[h][j : j + 1, :]
    full = [jnp.where(same_sub, jnp.concatenate([inv[h]] * (T // SUB), axis=0), 0.0) for h in range(HV)]
    for shift in (4, 5, 6):
        cut = ((row >> (shift + 1)) == (lane >> (shift + 1))) & ((row >> shift) != (lane >> shift)) & strict
        fb = [full[h].astype(BF) for h in range(HV)]
        m1 = [mm(jnp.where(cut, low[h], 0.0).astype(BF), fb[h]).astype(BF) for h in range(HV)]
        full = [full[h] - mm(fb[h], m1[h]) for h in range(HV)]

    uw = []
    for h in range(HV):
        beta = bcol[h]
        right = jnp.concatenate(
            [(beta * values[h]).astype(BF), (beta * dcol[h] * keys[h // 2]).astype(BF)], axis=1
        )
        uw.append(mm(full[h].astype(BF), right).astype(BF))
    eye = (row == lane).astype(F32)
    for h in range(HV):
        mu = mm((keys_t[h // 2] * f_row[h]).astype(BF), uw[h])
        psend[h] = jnp.concatenate([eye * d_last[h] - mu[:, W:], mu[:, :W]], axis=1).astype(BF)

    c_x = [
        send(2 + d, psend.at[lax.rem(x + d, NX)], pbuf.at[1, x], rs_x.at[d - 1], at_zx(0, d))
        for d in (1, 2, 3)
    ]
    c_z = [
        copy(6 + d, psend.at[lax.rem(x + d, NX)], pbuf.at[0, x], rs_z.at[d], at_zx(1, d))
        for d in range(NX)
    ]
    sends += [(z < NZ - 1, cp) for cp in c_z]

    @pl.when(z < NZ - 1)
    def _():
        for d in range(NX):
            pl.semaphore_wait(ready_1.at[d], 1)
            c_z[d].start()

    pbuf[1, x] = psend[x]


    @pl.when(c > 0)
    def _():
        c_hq.wait_recv()

    ext[0:8, 256:512] = hq[...].astype(F32)[8:16]
    queries = [unit(conv(256, cq, n * W)) * W ** -0.5 for n in range(HK)]
    scores = [mm_t(queries[n].astype(BF), keys_b[n]) for n in range(HK)]
    gate = sg[...]
    sg[...] = gate / (1.0 + jnp.exp(-gate))
    for h in range(HV):
        n = h // 2
        oq = mm((dm[h] * scores[n]).astype(BF), uw[h])
        o1[h] = oq[:, :W]
        qt[h] = (dcol[h] * queries[n] - oq[:, W:]).astype(BF)

    for cp in c_x:
        cp.wait_recv()

    def joined(later, earlier):
        r = mm(later[:, :W], earlier)
        return jnp.concatenate([r[:, :W], r[:, W:] + later[:, W:].astype(F32)], axis=1).astype(BF)

    own = [pbuf[1, b] for b in range(NX)]
    c10 = joined(own[1], own[0])
    c32 = joined(own[3], own[2])
    c210 = joined(own[2], c10)
    c3210 = joined(c32, c10)

    @pl.when(z > 0)
    def _():
        for cp in c_z:
            cp.wait_recv()

    prv = [pbuf[0, b] for b in range(NX)]
    p10 = joined(prv[1], prv[0])
    p32 = joined(prv[3], prv[2])
    p3210 = joined(p32, p10)
    two = joined(c3210, p3210)
    qs[0] = two[:, :W]
    qs[1] = two[:, W:]
    c_b3 = copy(11, qs.at[1], rb_u, rs_b.at[1], at_zx(3, 0))
    c_b1 = copy(10, qs, rb_mu, rs_b.at[0], at_zx(1, 0))
    sends += [(z < NZ - 3, c_b3), (z < NZ - 1, c_b1)]

    @pl.when(z < NZ - 3)
    def _():
        pl.semaphore_wait(ready_3, 1)
        c_b3.start()

    send_if(z < NZ - 1, c_b1)

    @pl.when(z > 0)
    def _():
        c_b1.wait_recv()

    @pl.when(z > 2)
    def _():
        c_b3.wait_recv()

    enter = (mm(rb_mu[0], rb_u[...]) + rb_mu[1].astype(F32)).astype(BF)
    ssend[0] = enter
    for b, pair in ((1, own[0]), (2, c10), (3, c210)):
        ssend[b] = (mm(pair[:, :W], enter) + pair[:, W:].astype(F32)).astype(BF)
    c_r = [
        send(11 + d, ssend.at[lax.rem(x + d, NX)], srecv.at[x], rs_r.at[d - 1], at_zx(0, d))
        for d in (1, 2, 3)
    ]
    srecv[x] = ssend[x]
    for cp in c_r:
        cp.wait_recv()

    for h in range(HV):
        o = o1[h] + mm(qt[h], srecv[h])
        o = o * lax.rsqrt(jnp.mean(o * o, axis=-1, keepdims=True) + 1e-6)
        yb[:, h * W : (h + 1) * W] = (o * sg[:, h * W : (h + 1) * W]).astype(BF)
    l_wo.wait()
    cw = D // NCH
    c_c = []
    for n in range(NCH):
        part = mm(yb[...], wo[:, n * cw : (n + 1) * cw]).astype(BF)
        for k in range(2 * NY):
            pm[n, k % 2, k // 2] = part[k * 16 : (k + 1) * 16]
        c_c.append(send(15 + n, pm.at[n, 1 - co], rc.at[n], rs_c.at[n], partner))
    c_y = []
    for n in range(NCH):
        c_c[n].wait_recv()
        s2[n] = (pm[n, co].astype(F32) + rc[n].astype(F32)).astype(BF)
        c_y.append([
            send(15 + NCH + 3 * n + d - 1, s2.at[n, lax.rem(y + d, NY)], ry.at[n, d - 1], rs_y.at[n, d - 1], at_y(d))
            for d in (1, 2, 3)
        ])
    for n in range(NCH):
        for cp in c_y[n]:
            cp.wait_recv()
        tot = pm[n, co, y].astype(F32) + rc[n, y].astype(F32)
        for d in range(3):
            tot = tot + ry[n, d].astype(F32)
        out_ref[:, n * cw : (n + 1) * cw] = tot.astype(BF)
    for cond, cp in sends:
        if cond is None:
            cp.wait_send()
        else:
            pl.when(cond)(cp.wait_send)


def per_device(*args):
    vm = pltpu.VMEM
    dma = pltpu.SemaphoreType.DMA
    any_spec = pl.BlockSpec(memory_space=pl.ANY)
    return pl.pallas_call(
        kernel,
        out_shape=pltpu.VMEM((16, D), BF),
        in_specs=[any_spec] * 13,
        out_specs=pl.BlockSpec(memory_space=pltpu.VMEM),
        scratch_shapes=[
            vm((T, D), BF), vm((D, 256), BF), vm((D, 256), BF), vm((D, 512), BF), vm((D, 512), BF),
            vm((512, D), BF), vm((4, 256), BF), vm((4, 256), BF), vm((4, 512), BF),
            vm((HV, T), F32), vm((HV, T), F32), pltpu.SMEM((DOCS,), jnp.int32), pltpu.SMEM((HV,), F32),
            vm((T, 256), BF), vm((T, 256), BF), vm((T, 512), BF),
            vm((16, 256), BF), vm((16, 256), BF), vm((16, 512), BF),
            vm((T + 8, 1024), F32), vm((2 * HV, T), F32),
            vm((HV, T, T), F32), vm((HV, T, T), F32), vm((HV, T, T), F32), vm((HV, T, T), F32),
            vm((T, (SUB - 1) * T), BF),
            vm((T, 512), F32),
            vm((HV, W, 2 * W), BF), vm((2, NX, W, 2 * W), BF),
            vm((HV, T, W), F32), vm((HV, T, W), BF),
            vm((2, W, W), BF), vm((2, W, W), BF), vm((W, W), BF),
            vm((NX, W, W), BF), vm((HV, W, W), BF),
            vm((T, 512), BF),
            vm((NCH, 2, NY, 16, D // NCH), BF), vm((NCH, NY, 16, D // NCH), BF),
            vm((NCH, NY, 16, D // NCH), BF), vm((NCH, 3, 16, D // NCH), BF),
            pltpu.SemaphoreType.REGULAR, pltpu.SemaphoreType.REGULAR((NX,)), pltpu.SemaphoreType.REGULAR,
            dma((13,)), dma((15 + NCH * 4,)), dma((3,)), dma((3,)), dma((4,)), dma((2,)), dma((3,)),
            dma((NCH,)), dma((NCH, 3)),
        ],
        name="layer",
        compiler_params=pltpu.CompilerParams(
            collective_id=0, has_side_effects=True, vmem_limit_bytes=56 << 20
        ),
    )(*args)


def solution(mesh):
    in_specs = (
        P("ctx", None),
        P(),
        P(None, "head"),
        P(None, "head"),
        P(None, "head"),
        P(None, "head"),
        P(None, "head"),
        P(None, "head"),
        P(None, "head"),
        P("head", "ctx"),
        P("head", "ctx"),
        P("head"),
        P("head", None),
    )
    out_specs = P(("ctx", "head"), None)
    return jax.shard_map(
        per_device, mesh=mesh, in_specs=in_specs, out_specs=out_specs, check_vma=False
    )
```

```python
import jax
import jax.numpy as jnp
from jax import lax
from jax.experimental import pallas as pl
from jax.experimental.pallas import tpu as pltpu
from jax.sharding import PartitionSpec as P

MESH = pl.DeviceIdType.MESH
F32 = jnp.float32
BF = jnp.bfloat16
T = 128
W = 128
NX = 4
NZ = 8
NY = 4
HV = 4
HK = 2
DOCS = 16
SUB = 16
NCH = 1
D = 2048


def mm(a, b):
    return jnp.dot(a, b, preferred_element_type=F32)


def mm_t(a, b):
    return lax.dot_general(a, b, (((1,), (1,)), ((), ())), preferred_element_type=F32)


def iota(shape, dim):
    return lax.broadcasted_iota(jnp.int32, shape, dim)


def kernel(
    tok_h, doc_h, wq_h, wk_h, wv_h, wg_h, cq_h, ck_h, cv_h, bl_h, dl_h, al_h, wo_h,
    out_ref,
    tok, wq, wk, wv, wg, wo, cq, ck, cv, bl, dl, doc_s, al_s,
    pk, pq, pv, hk, hq, hv, ext, sc8, dm, bdm, dcol, bcol, pick,
    sg, psend, pbuf, o1, qt, qs, rb_mu, rb_u, ssend, srecv, yb, pm, rc, s2, ry,
    ready_1, ready_3, lsem, ss, rs_halo, rs_x, rs_z, rs_b, rs_r, rs_c, rs_y,
):
    c = lax.axis_index("ctx")
    hd = lax.axis_index("head")
    z, x = c // NX, c % NX
    y, co = hd // 2, hd % 2

    def at_zx(dz, dx):
        return (lax.rem(z + dz + NZ, NZ) * NX + lax.rem(x + dx, NX), hd)

    def at_y(dy):
        return (c, lax.rem(y + dy, NY) * 2 + co)

    partner = (c, y * 2 + 1 - co)

    def load(i, src, dst):
        cp = pltpu.make_async_copy(src, dst, lsem.at[i])
        cp.start()
        return cp

    l_doc = load(0, doc_h, doc_s)
    l_al = load(1, al_h, al_s)
    l_bl = load(2, bl_h, bl)
    l_dl = load(3, dl_h, dl)
    l_tok = load(4, tok_h, tok)
    l_wk = load(5, wk_h, wk)
    l_wv = load(7, wv_h, wv)

    barrier = pltpu.get_barrier_semaphore()

    def hello(sem, dev):
        pl.semaphore_signal(sem, inc=1, device_id=dev, device_id_type=MESH)

    mates = [at_zx(0, d) for d in (1, 2, 3)] + [partner] + [at_y(d) for d in (1, 2, 3)]
    for dev in mates:
        hello(barrier, dev)

    @pl.when((z > 0) & (x == 0))
    def _():
        hello(barrier, at_zx(-1, NX - 1))

    @pl.when(z < NZ - 1)
    def _():
        for d in range(NX):
            hello(barrier, at_zx(1, d))

    @pl.when(z < NZ - 3)
    def _():
        hello(barrier, at_zx(3, 0))

    l_ck = load(8, ck_h, ck)
    l_cv = load(10, cv_h, cv)
    l_wq = load(6, wq_h, wq)
    l_cq = load(9, cq_h, cq)
    l_wg = load(11, wg_h, wg)
    l_wo = load(12, wo_h, wo)

    l_doc.wait()
    l_al.wait()
    l_bl.wait()
    l_dl.wait()
    base = c * T
    offs = []
    total = jnp.int32(0)
    for j in range(DOCS):
        offs.append(total)
        total = total + doc_s[j]
    row = iota((T, T), 0)
    lane = iota((T, T), 1)
    start = jnp.zeros((T, T), jnp.int32)
    start_last = jnp.int32(0)
    for j in range(1, DOCS):
        start = jnp.where(offs[j] <= row + base, offs[j], start)
        start_last = jnp.where(offs[j] <= base + T - 1, offs[j], start_last)
    age = row + base - start
    kept = start < base
    lower = (lane <= row) & (base + lane >= start)
    strict = lane < row
    dlv = dl[...]
    soft = jnp.maximum(dlv, 0.0) + jnp.log(1.0 + jnp.exp(-jnp.abs(dlv)))
    r4 = iota((HV, T), 0)
    rate = jnp.where(r4 == 0, al_s[0], jnp.where(r4 == 1, al_s[1], jnp.where(r4 == 2, al_s[2], al_s[3])))
    sc8[0:HV] = -jnp.exp(rate) * soft
    sc8[HV : 2 * HV] = 1.0 / (1.0 + jnp.exp(-bl[...]))
    both = sc8[...]
    upper = (row <= lane).astype(F32)
    cum = jnp.dot(both, upper, preferred_element_type=F32, precision=lax.Precision.HIGHEST)
    both = jnp.where(iota((2 * HV, T), 0) < HV, cum, both)
    cols = jnp.transpose(both)
    f_row, d_last = [], []
    for h in range(HV):
        gcol = jnp.broadcast_to(cols[:, h : h + 1], (T, T))
        grow = both[h : h + 1, :]
        decay = jnp.exp(jnp.where(lower, gcol - grow, -1e30))
        beta = jnp.broadcast_to(cols[:, HV + h : HV + h + 1], (T, T))
        into = jnp.where(kept, jnp.exp(gcol), 0.0)
        dm[h] = decay
        bdm[h] = jnp.where(strict, decay * beta, 0.0)
        dcol[h] = into
        bcol[h] = beta
        f_row.append(
            jnp.where(
                iota((1, T), 1) + base >= start_last, jnp.exp(gcol[T - 1 : T, :] - grow), 0.0
            )
        )
        d_last.append(into[T - 1 : T, :])
    same_sub = (row >> 4) == (lane >> 4)
    for j in range(SUB - 1):
        pick[:, j * T : (j + 1) * T] = (same_sub & ((row & 15) == j)).astype(F32).astype(BF)

    @pl.when(c == 0)
    def _():
        hk[...] = jnp.zeros_like(hk)
        hq[...] = jnp.zeros_like(hq)
        hv[...] = jnp.zeros_like(hv)

    @pl.when(z == 0)
    def _():
        pbuf[0] = jnp.zeros((NX, W, 2 * W), BF)
        rb_mu[...] = jnp.zeros_like(rb_mu)

    @pl.when(z < 3)
    def _():
        rb_u[...] = jnp.zeros_like(rb_u)

    nxt = (lax.rem(c + 1, NX * NZ), hd)
    sends = []

    def copy(i, src, dst, recv, dev):
        return pltpu.make_async_remote_copy(
            src_ref=src, dst_ref=dst, send_sem=ss.at[i], recv_sem=recv,
            device_id=dev, device_id_type=MESH,
        )

    def send(i, src, dst, recv, dev):
        cp = copy(i, src, dst, recv, dev)
        cp.start()
        sends.append((None, cp))
        return cp

    def send_if(cond, cp):
        @pl.when(cond)
        def _():
            cp.start()

    c_hk = copy(0, pk.at[T - 16 : T], hk, rs_halo.at[0], nxt)
    c_hq = copy(1, pq.at[T - 16 : T], hq, rs_halo.at[1], nxt)
    c_hv = copy(2, pv.at[T - 16 : T], hv, rs_halo.at[2], nxt)
    sends += [(c < NX * NZ - 1, cp) for cp in (c_hk, c_hq, c_hv)]
    more = c < NX * NZ - 1
    l_tok.wait()
    l_wk.wait()
    pk[...] = mm(tok[...], wk[...]).astype(BF)

    earlier = jnp.where(z > 0, NX, 0) + jnp.where(z > 2, 1, 0)
    after = jnp.where((z < NZ - 1) & (x == NX - 1), 1, 0)
    pl.semaphore_wait(barrier, len(mates) + earlier + after)

    @pl.when(z > 0)
    def _():
        for d in range(NX):
            hello(ready_1.at[(NX - d) % NX], at_zx(-1, d))

    @pl.when(z > 2)
    def _():
        hello(ready_3, at_zx(-3, 0))

    send_if(more, c_hk)
    l_wv.wait()
    pv[...] = mm(tok[...], wv[...]).astype(BF)
    send_if(more, c_hv)
    l_wq.wait()
    pq[...] = mm(tok[...], wq[...]).astype(BF)
    send_if(more, c_hq)

    l_wg.wait()
    sg[...] = mm(tok[...], wg[...]).astype(BF).astype(F32)

    ext[8 : 8 + T, 0:256] = pk[...].astype(F32)
    ext[8 : 8 + T, 256:512] = pq[...].astype(F32)
    ext[8 : 8 + T, 512:1024] = pv[...].astype(F32)
    l_ck.wait()
    l_cv.wait()
    l_cq.wait()

    def conv(first, taps, col):
        wide = slice(first + col, first + col + W)
        w = taps[...].astype(F32)[:, col : col + W]
        acc = w[3:4] * ext[8 : 8 + T, wide]
        for s in (1, 2, 3):
            acc = acc + jnp.where(age >= s, w[3 - s : 4 - s] * ext[8 - s : 8 - s + T, wide], 0.0)
        return acc / (1.0 + jnp.exp(-acc))

    def unit(a):
        return a * lax.rsqrt(jnp.sum(a * a, axis=-1, keepdims=True) + 1e-6)


    @pl.when(c > 0)
    def _():
        c_hk.wait_recv()

    ext[0:8, 0:256] = hk[...].astype(F32)[8:16]
    keys = [unit(conv(0, ck, n * W)) for n in range(HK)]
    keys_b = [k.astype(BF) for k in keys]
    keys_t = [jnp.transpose(k) for k in keys]
    grams = [mm_t(k, k) for k in keys_b]

    @pl.when(c > 0)
    def _():
        c_hv.wait_recv()

    ext[0:8, 512:1024] = hv[...].astype(F32)[8:16]
    values = [conv(512, cv, h * W) for h in range(HV)]

    low = [bdm[h] * grams[h // 2] for h in range(HV)]
    packed = []
    lane16 = iota((SUB, T), 1)
    for h in range(HV):
        p = None
        for b in range(T // SUB):
            q = jnp.where((lane16 >> 4) == b, low[h][b * SUB : (b + 1) * SUB], 0.0)
            p = q if p is None else p + q
        packed.append(p)
    coef = mm(jnp.concatenate(packed, axis=0).astype(BF), pick[...])
    inv = [(iota((SUB, T), 0) == (lane16 & 15)).astype(F32) for _ in range(HV)]
    for j in range(SUB - 1):
        for h in range(HV):
            cj = coef[h * SUB : (h + 1) * SUB, j * T : (j + 1) * T]
            inv[h] = inv[h] - cj * inv[h][j : j + 1, :]
    full = [jnp.where(same_sub, jnp.concatenate([inv[h]] * (T // SUB), axis=0), 0.0) for h in range(HV)]
    for shift in (4, 5, 6):
        cut = ((row >> (shift + 1)) == (lane >> (shift + 1))) & ((row >> shift) != (lane >> shift)) & strict
        fb = [full[h].astype(BF) for h in range(HV)]
        m1 = [mm(jnp.where(cut, low[h], 0.0).astype(BF), fb[h]).astype(BF) for h in range(HV)]
        full = [full[h] - mm(fb[h], m1[h]) for h in range(HV)]

    uw = []
    for h in range(HV):
        beta = bcol[h]
        right = jnp.concatenate(
            [(beta * values[h]).astype(BF), (beta * dcol[h] * keys[h // 2]).astype(BF)], axis=1
        )
        uw.append(mm(full[h].astype(BF), right).astype(BF))
    eye = (row == lane).astype(F32)
    for h in range(HV):
        mu = mm((keys_t[h // 2] * f_row[h]).astype(BF), uw[h])
        psend[h] = jnp.concatenate([eye * d_last[h] - mu[:, W:], mu[:, :W]], axis=1).astype(BF)

    c_x = [
        send(2 + d, psend.at[lax.rem(x + d, NX)], pbuf.at[1, x], rs_x.at[d - 1], at_zx(0, d))
        for d in (1, 2, 3)
    ]
    c_z = [
        copy(6 + d, psend.at[lax.rem(x + d, NX)], pbuf.at[0, x], rs_z.at[d], at_zx(1, d))
        for d in range(NX)
    ]
    sends += [(z < NZ - 1, cp) for cp in c_z]

    @pl.when(z < NZ - 1)
    def _():
        for d in range(NX):
            pl.semaphore_wait(ready_1.at[d], 1)
            c_z[d].start()

    pbuf[1, x] = psend[x]


    @pl.when(c > 0)
    def _():
        c_hq.wait_recv()

    ext[0:8, 256:512] = hq[...].astype(F32)[8:16]
    queries = [unit(conv(256, cq, n * W)) * W ** -0.5 for n in range(HK)]
    scores = [mm_t(queries[n].astype(BF), keys_b[n]) for n in range(HK)]
    gate = sg[...]
    sg[...] = gate / (1.0 + jnp.exp(-gate))
    for h in range(HV):
        n = h // 2
        oq = mm((dm[h] * scores[n]).astype(BF), uw[h])
        o1[h] = oq[:, :W]
        qt[h] = (dcol[h] * queries[n] - oq[:, W:]).astype(BF)

    for cp in c_x:
        cp.wait_recv()

    def joined(later, earlier):
        r = mm(later[:, :W], earlier)
        return jnp.concatenate([r[:, :W], r[:, W:] + later[:, W:].astype(F32)], axis=1).astype(BF)

    own = [pbuf[1, b] for b in range(NX)]
    c10 = joined(own[1], own[0])
    c32 = joined(own[3], own[2])
    c210 = joined(own[2], c10)
    c3210 = joined(c32, c10)

    @pl.when(z > 0)
    def _():
        for cp in c_z:
            cp.wait_recv()

    prv = [pbuf[0, b] for b in range(NX)]
    p10 = joined(prv[1], prv[0])
    p32 = joined(prv[3], prv[2])
    p3210 = joined(p32, p10)
    two = joined(c3210, p3210)
    qs[0] = two[:, :W]
    qs[1] = two[:, W:]
    c_b3 = copy(11, qs.at[1], rb_u, rs_b.at[1], at_zx(3, 0))
    c_b1 = copy(10, qs, rb_mu, rs_b.at[0], at_zx(1, 0))
    sends += [(z < NZ - 3, c_b3), (z < NZ - 1, c_b1)]

    @pl.when(z < NZ - 3)
    def _():
        pl.semaphore_wait(ready_3, 1)
        c_b3.start()

    send_if(z < NZ - 1, c_b1)

    @pl.when(z > 0)
    def _():
        c_b1.wait_recv()

    @pl.when(z > 2)
    def _():
        c_b3.wait_recv()

    enter = (mm(rb_mu[0], rb_u[...]) + rb_mu[1].astype(F32)).astype(BF)
    ssend[0] = enter
    for b, pair in ((1, own[0]), (2, c10), (3, c210)):
        ssend[b] = (mm(pair[:, :W], enter) + pair[:, W:].astype(F32)).astype(BF)
    c_r = [
        send(11 + d, ssend.at[lax.rem(x + d, NX)], srecv.at[x], rs_r.at[d - 1], at_zx(0, d))
        for d in (1, 2, 3)
    ]
    srecv[x] = ssend[x]
    for cp in c_r:
        cp.wait_recv()

    for h in range(HV):
        o = o1[h] + mm(qt[h], srecv[h])
        o = o * lax.rsqrt(jnp.mean(o * o, axis=-1, keepdims=True) + 1e-6)
        yb[:, h * W : (h + 1) * W] = (o * sg[:, h * W : (h + 1) * W]).astype(BF)
    l_wo.wait()
    cw = D // NCH
    c_c = []
    for n in range(NCH):
        part = mm(yb[...], wo[:, n * cw : (n + 1) * cw]).astype(BF)
        for k in range(2 * NY):
            pm[n, k % 2, k // 2] = part[k * 16 : (k + 1) * 16]
        c_c.append(send(15 + n, pm.at[n, 1 - co], rc.at[n], rs_c.at[n], partner))
    c_y = []
    for n in range(NCH):
        c_c[n].wait_recv()
        s2[n] = (pm[n, co].astype(F32) + rc[n].astype(F32)).astype(BF)
        c_y.append([
            send(15 + NCH + 3 * n + d - 1, s2.at[n, lax.rem(y + d, NY)], ry.at[n, d - 1], rs_y.at[n, d - 1], at_y(d))
            for d in (1, 2, 3)
        ])
    for n in range(NCH):
        for cp in c_y[n]:
            cp.wait_recv()
        tot = pm[n, co, y].astype(F32) + rc[n, y].astype(F32)
        for d in range(3):
            tot = tot + ry[n, d].astype(F32)
        out_ref[:, n * cw : (n + 1) * cw] = tot.astype(BF)
    for cond, cp in sends:
        if cond is None:
            cp.wait_send()
        else:
            pl.when(cond)(cp.wait_send)


def per_device(*args):
    vm = pltpu.VMEM
    dma = pltpu.SemaphoreType.DMA
    any_spec = pl.BlockSpec(memory_space=pl.ANY)
    return pl.pallas_call(
        kernel,
        out_shape=pltpu.VMEM((16, D), BF),
        in_specs=[any_spec] * 13,
        out_specs=pl.BlockSpec(memory_space=pltpu.VMEM),
        scratch_shapes=[
            vm((T, D), BF), vm((D, 256), BF), vm((D, 256), BF), vm((D, 512), BF), vm((D, 512), BF),
            vm((512, D), BF), vm((4, 256), BF), vm((4, 256), BF), vm((4, 512), BF),
            vm((HV, T), F32), vm((HV, T), F32), pltpu.SMEM((DOCS,), jnp.int32), pltpu.SMEM((HV,), F32),
            vm((T, 256), BF), vm((T, 256), BF), vm((T, 512), BF),
            vm((16, 256), BF), vm((16, 256), BF), vm((16, 512), BF),
            vm((T + 8, 1024), F32), vm((2 * HV, T), F32),
            vm((HV, T, T), F32), vm((HV, T, T), F32), vm((HV, T, T), F32), vm((HV, T, T), F32),
            vm((T, (SUB - 1) * T), BF),
            vm((T, 512), F32),
            vm((HV, W, 2 * W), BF), vm((2, NX, W, 2 * W), BF),
            vm((HV, T, W), F32), vm((HV, T, W), BF),
            vm((2, W, W), BF), vm((2, W, W), BF), vm((W, W), BF),
            vm((NX, W, W), BF), vm((HV, W, W), BF),
            vm((T, 512), BF),
            vm((NCH, 2, NY, 16, D // NCH), BF), vm((NCH, NY, 16, D // NCH), BF),
            vm((NCH, NY, 16, D // NCH), BF), vm((NCH, 3, 16, D // NCH), BF),
            pltpu.SemaphoreType.REGULAR((NX,)), pltpu.SemaphoreType.REGULAR,
            dma((13,)), dma((15 + NCH * 4,)), dma((3,)), dma((3,)), dma((4,)), dma((2,)), dma((3,)),
            dma((NCH,)), dma((NCH, 3)),
        ],
        name="layer",
        compiler_params=pltpu.CompilerParams(
            collective_id=0, has_side_effects=True, vmem_limit_bytes=56 << 20
        ),
    )(*args)


def solution(mesh):
    in_specs = (
        P("ctx", None),
        P(),
        P(None, "head"),
        P(None, "head"),
        P(None, "head"),
        P(None, "head"),
        P(None, "head"),
        P(None, "head"),
        P(None, "head"),
        P("head", "ctx"),
        P("head", "ctx"),
        P("head"),
        P("head", None),
    )
    out_specs = P(("ctx", "head"), None)
    return jax.shard_map(
        per_device, mesh=mesh, in_specs=in_specs, out_specs=out_specs, check_vma=False
    )
```

```python
import jax
import jax.numpy as jnp
from jax import lax
from jax.experimental import pallas as pl
from jax.experimental.pallas import tpu as pltpu
from jax.sharding import PartitionSpec as P

MESH = pl.DeviceIdType.MESH
F32 = jnp.float32
BF = jnp.bfloat16
T = 128
W = 128
NX = 4
NZ = 8
NY = 4
HV = 4
HK = 2
DOCS = 16
SUB = 16
NCH = 1
D = 2048


def mm(a, b):
    return jnp.dot(a, b, preferred_element_type=F32)


def mm_t(a, b):
    return lax.dot_general(a, b, (((1,), (1,)), ((), ())), preferred_element_type=F32)


def iota(shape, dim):
    return lax.broadcasted_iota(jnp.int32, shape, dim)


def kernel(
    tok_h, doc_h, wq_h, wk_h, wv_h, wg_h, cq_h, ck_h, cv_h, bl_h, dl_h, al_h, wo_h,
    out_ref,
    tok, wq, wk, wv, wg, wo, cq, ck, cv, bl, dl, doc_s, al_s,
    pk, pq, pv, hk, hq, hv, ext, sc8, dm, bdm, dcol, bcol, pick,
    sg, psend, pbuf, o1, qt, qs, rb_mu, rb_u, ssend, srecv, yb, pm, rc, s2, ry,
    ready_1, ready_3, lsem, ss, rs_halo, rs_x, rs_z, rs_b, rs_r, rs_c, rs_y,
):
    c = lax.axis_index("ctx")
    hd = lax.axis_index("head")
    z, x = c // NX, c % NX
    y, co = hd // 2, hd % 2

    def at_zx(dz, dx):
        return (lax.rem(z + dz + NZ, NZ) * NX + lax.rem(x + dx, NX), hd)

    def at_y(dy):
        return (c, lax.rem(y + dy, NY) * 2 + co)

    partner = (c, y * 2 + 1 - co)

    def load(i, src, dst):
        cp = pltpu.make_async_copy(src, dst, lsem.at[i])
        cp.start()
        return cp

    l_doc = load(0, doc_h, doc_s)
    l_al = load(1, al_h, al_s)
    l_bl = load(2, bl_h, bl)
    l_dl = load(3, dl_h, dl)
    l_tok = load(4, tok_h, tok)
    l_wk = load(5, wk_h, wk)
    l_wv = load(7, wv_h, wv)

    barrier = pltpu.get_barrier_semaphore()

    def hello(sem, dev):
        pl.semaphore_signal(sem, inc=1, device_id=dev, device_id_type=MESH)

    mates = [at_zx(0, d) for d in (1, 2, 3)] + [partner] + [at_y(d) for d in (1, 2, 3)]
    for dev in mates:
        hello(barrier, dev)

    @pl.when((z > 0) & (x == 0))
    def _():
        hello(barrier, at_zx(-1, NX - 1))

    @pl.when(z < NZ - 1)
    def _():
        for d in range(NX):
            hello(barrier, at_zx(1, d))

    @pl.when(z < NZ - 3)
    def _():
        hello(barrier, at_zx(3, 0))

    l_ck = load(8, ck_h, ck)
    l_cv = load(10, cv_h, cv)
    l_wq = load(6, wq_h, wq)
    l_cq = load(9, cq_h, cq)
    l_wg = load(11, wg_h, wg)
    l_wo = load(12, wo_h, wo)

    l_doc.wait()
    l_al.wait()
    l_bl.wait()
    l_dl.wait()
    base = c * T
    offs = []
    total = jnp.int32(0)
    for j in range(DOCS):
        offs.append(total)
        total = total + doc_s[j]
    row = iota((T, T), 0)
    lane = iota((T, T), 1)
    start = jnp.zeros((T, T), jnp.int32)
    start_last = jnp.int32(0)
    for j in range(1, DOCS):
        start = jnp.where(offs[j] <= row + base, offs[j], start)
        start_last = jnp.where(offs[j] <= base + T - 1, offs[j], start_last)
    age = row + base - start
    kept = start < base
    lower = (lane <= row) & (base + lane >= start)
    strict = lane < row
    dlv = dl[...]
    soft = jnp.maximum(dlv, 0.0) + jnp.log(1.0 + jnp.exp(-jnp.abs(dlv)))
    r4 = iota((HV, T), 0)
    rate = jnp.where(r4 == 0, al_s[0], jnp.where(r4 == 1, al_s[1], jnp.where(r4 == 2, al_s[2], al_s[3])))
    sc8[0:HV] = -jnp.exp(rate) * soft
    sc8[HV : 2 * HV] = 1.0 / (1.0 + jnp.exp(-bl[...]))
    both = sc8[...]
    upper = (row <= lane).astype(F32)
    cum = jnp.dot(both, upper, preferred_element_type=F32, precision=lax.Precision.HIGHEST)
    both = jnp.where(iota((2 * HV, T), 0) < HV, cum, both)
    cols = jnp.transpose(both)
    f_row, d_last = [], []
    for h in range(HV):
        gcol = jnp.broadcast_to(cols[:, h : h + 1], (T, T))
        grow = both[h : h + 1, :]
        decay = jnp.exp(jnp.where(lower, gcol - grow, -1e30))
        beta = jnp.broadcast_to(cols[:, HV + h : HV + h + 1], (T, T))
        into = jnp.where(kept, jnp.exp(gcol), 0.0)
        dm[h] = decay
        bdm[h] = jnp.where(strict, decay * beta, 0.0)
        dcol[h] = into
        bcol[h] = beta
        f_row.append(
            jnp.where(
                iota((1, T), 1) + base >= start_last, jnp.exp(gcol[T - 1 : T, :] - grow), 0.0
            )
        )
        d_last.append(into[T - 1 : T, :])
    same_sub = (row >> 4) == (lane >> 4)
    for j in range(SUB - 1):
        pick[:, j * T : (j + 1) * T] = (same_sub & ((row & 15) == j)).astype(F32).astype(BF)

    @pl.when(c == 0)
    def _():
        hk[...] = jnp.zeros_like(hk)
        hq[...] = jnp.zeros_like(hq)
        hv[...] = jnp.zeros_like(hv)

    @pl.when(z == 0)
    def _():
        pbuf[0] = jnp.zeros((NX, W, 2 * W), BF)
        rb_mu[...] = jnp.zeros_like(rb_mu)

    @pl.when(z < 3)
    def _():
        rb_u[...] = jnp.zeros_like(rb_u)

    nxt = (lax.rem(c + 1, NX * NZ), hd)
    sends = []

    def copy(i, src, dst, recv, dev):
        return pltpu.make_async_remote_copy(
            src_ref=src, dst_ref=dst, send_sem=ss.at[i], recv_sem=recv,
            device_id=dev, device_id_type=MESH,
        )

    def send(i, src, dst, recv, dev):
        cp = copy(i, src, dst, recv, dev)
        cp.start()
        sends.append((None, cp))
        return cp

    def send_if(cond, cp):
        @pl.when(cond)
        def _():
            cp.start()

    c_hk = copy(0, pk.at[T - 16 : T], hk, rs_halo.at[0], nxt)
    c_hq = copy(1, pq.at[T - 16 : T], hq, rs_halo.at[1], nxt)
    c_hv = copy(2, pv.at[T - 16 : T], hv, rs_halo.at[2], nxt)
    sends += [(c < NX * NZ - 1, cp) for cp in (c_hk, c_hq, c_hv)]
    more = c < NX * NZ - 1
    l_tok.wait()
    l_wk.wait()
    pk[...] = mm(tok[...], wk[...]).astype(BF)

    earlier = jnp.where(z > 0, NX, 0) + jnp.where(z > 2, 1, 0)
    after = jnp.where((z < NZ - 1) & (x == NX - 1), 1, 0)
    pl.semaphore_wait(barrier, len(mates) + earlier + after)

    @pl.when(z > 0)
    def _():
        for d in range(NX):
            hello(ready_1.at[(NX - d) % NX], at_zx(-1, d))

    @pl.when(z > 2)
    def _():
        hello(ready_3, at_zx(-3, 0))

    send_if(more, c_hk)
    l_wv.wait()
    pv[...] = mm(tok[...], wv[...]).astype(BF)
    send_if(more, c_hv)
    l_wq.wait()
    pq[...] = mm(tok[...], wq[...]).astype(BF)
    send_if(more, c_hq)

    l_wg.wait()
    sg[...] = mm(tok[...], wg[...]).astype(BF).astype(F32)

    ext[8 : 8 + T, 0:256] = pk[...].astype(F32)
    ext[8 : 8 + T, 256:512] = pq[...].astype(F32)
    ext[8 : 8 + T, 512:1024] = pv[...].astype(F32)
    l_ck.wait()
    l_cv.wait()
    l_cq.wait()

    def conv(first, taps, col):
        wide = slice(first + col, first + col + W)
        w = taps[...].astype(F32)[:, col : col + W]
        acc = w[3:4] * ext[8 : 8 + T, wide]
        for s in (1, 2, 3):
            acc = acc + jnp.where(age >= s, w[3 - s : 4 - s] * ext[8 - s : 8 - s + T, wide], 0.0)
        return acc / (1.0 + jnp.exp(-acc))

    def unit(a):
        return a * lax.rsqrt(jnp.sum(a * a, axis=-1, keepdims=True) + 1e-6)


    @pl.when(c > 0)
    def _():
        c_hk.wait_recv()

    ext[0:8, 0:256] = hk[...].astype(F32)[8:16]
    keys = [unit(conv(0, ck, n * W)) for n in range(HK)]
    keys_b = [k.astype(BF) for k in keys]
    keys_t = [jnp.transpose(k) for k in keys]
    grams = [mm_t(k, k) for k in keys_b]

    @pl.when(c > 0)
    def _():
        c_hv.wait_recv()

    ext[0:8, 512:1024] = hv[...].astype(F32)[8:16]
    values = [conv(512, cv, h * W) for h in range(HV)]

    low = [bdm[h] * grams[h // 2] for h in range(HV)]
    packed = []
    lane16 = iota((SUB, T), 1)
    for h in range(HV):
        p = None
        for b in range(T // SUB):
            q = jnp.where((lane16 >> 4) == b, low[h][b * SUB : (b + 1) * SUB], 0.0)
            p = q if p is None else p + q
        packed.append(p)
    coef = mm(jnp.concatenate(packed, axis=0).astype(BF), pick[...])
    inv = [(iota((SUB, T), 0) == (lane16 & 15)).astype(F32) for _ in range(HV)]
    for j in range(SUB - 1):
        for h in range(HV):
            cj = coef[h * SUB : (h + 1) * SUB, j * T : (j + 1) * T]
            inv[h] = inv[h] - cj * inv[h][j : j + 1, :]
    full = [jnp.where(same_sub, jnp.concatenate([inv[h]] * (T // SUB), axis=0), 0.0) for h in range(HV)]
    for shift in (4, 5, 6):
        cut = ((row >> (shift + 1)) == (lane >> (shift + 1))) & ((row >> shift) != (lane >> shift)) & strict
        fb = [full[h].astype(BF) for h in range(HV)]
        m1 = [mm(jnp.where(cut, low[h], 0.0).astype(BF), fb[h]).astype(BF) for h in range(HV)]
        full = [full[h] - mm(fb[h], m1[h]) for h in range(HV)]

    uw = []
    for h in range(HV):
        beta = bcol[h]
        right = jnp.concatenate(
            [(beta * values[h]).astype(BF), (beta * dcol[h] * keys[h // 2]).astype(BF)], axis=1
        )
        uw.append(mm(full[h].astype(BF), right).astype(BF))
    eye = (row == lane).astype(F32)
    for h in range(HV):
        mu = mm((keys_t[h // 2] * f_row[h]).astype(BF), uw[h])
        psend[h] = jnp.concatenate([eye * d_last[h] - mu[:, W:], mu[:, :W]], axis=1).astype(BF)

    c_x = [
        send(2 + d, psend.at[lax.rem(x + d, NX)], pbuf.at[1, x], rs_x.at[d - 1], at_zx(0, d))
        for d in (1, 2, 3)
    ]
    c_z = [
        copy(6 + d, psend.at[lax.rem(x + d, NX)], pbuf.at[0, x], rs_z.at[d], at_zx(1, d))
        for d in range(NX)
    ]
    sends += [(z < NZ - 1, cp) for cp in c_z]

    @pl.when(z < NZ - 1)
    def _():
        for d in range(NX):
            pl.semaphore_wait(ready_1.at[d], 1)
            c_z[d].start()

    pbuf[1, x] = psend[x]


    @pl.when(c > 0)
    def _():
        c_hq.wait_recv()

    ext[0:8, 256:512] = hq[...].astype(F32)[8:16]
    queries = [unit(conv(256, cq, n * W)) * W ** -0.5 for n in range(HK)]
    scores = [mm_t(queries[n].astype(BF), keys_b[n]) for n in range(HK)]
    gate = sg[...]
    sg[...] = gate / (1.0 + jnp.exp(-gate))
    for h in range(HV):
        n = h // 2
        oq = mm((dm[h] * scores[n]).astype(BF), uw[h])
        o1[h] = oq[:, :W]
        qt[h] = (dcol[h] * queries[n] - oq[:, W:]).astype(BF)

    for cp in c_x:
        cp.wait_recv()

    def joined(later, earlier):
        r = mm(later[:, :W], earlier)
        return jnp.concatenate([r[:, :W], r[:, W:] + later[:, W:].astype(F32)], axis=1).astype(BF)

    own = [pbuf[1, b] for b in range(NX)]
    c10 = joined(own[1], own[0])
    c32 = joined(own[3], own[2])
    c210 = joined(own[2], c10)
    c3210 = joined(c32, c10)

    @pl.when(z > 0)
    def _():
        for cp in c_z:
            cp.wait_recv()

    prv = [pbuf[0, b] for b in range(NX)]
    p10 = joined(prv[1], prv[0])
    p32 = joined(prv[3], prv[2])
    p3210 = joined(p32, p10)
    qs[1] = (mm(c3210[:, :W], p3210[:, W:]) + c3210[:, W:].astype(F32)).astype(BF)
    c_b3 = copy(11, qs.at[1], rb_u, rs_b.at[1], at_zx(3, 0))
    c_b1 = copy(10, qs.at[1], rb_mu.at[1], rs_b.at[0], at_zx(1, 0))
    c_b0 = copy(15 + 4 * NCH, qs.at[0], rb_mu.at[0], rs_b.at[2], at_zx(1, 0))
    sends += [(z < NZ - 3, c_b3), (z < NZ - 1, c_b1), (z < NZ - 1, c_b0)]

    @pl.when(z < NZ - 3)
    def _():
        pl.semaphore_wait(ready_3, 1)
        c_b3.start()

    qs[0] = mm(c3210[:, :W], p3210[:, :W]).astype(BF)

    @pl.when(z < NZ - 1)
    def _():
        c_b0.start()
        c_b1.start()

    @pl.when(z > 0)
    def _():
        c_b0.wait_recv()
        c_b1.wait_recv()

    @pl.when(z > 2)
    def _():
        c_b3.wait_recv()

    enter = (mm(rb_mu[0], rb_u[...]) + rb_mu[1].astype(F32)).astype(BF)
    ssend[0] = enter
    for b, pair in ((1, own[0]), (2, c10), (3, c210)):
        ssend[b] = (mm(pair[:, :W], enter) + pair[:, W:].astype(F32)).astype(BF)
    c_r = [
        send(11 + d, ssend.at[lax.rem(x + d, NX)], srecv.at[x], rs_r.at[d - 1], at_zx(0, d))
        for d in (1, 2, 3)
    ]
    srecv[x] = ssend[x]
    for cp in c_r:
        cp.wait_recv()

    for h in range(HV):
        o = o1[h] + mm(qt[h], srecv[h])
        o = o * lax.rsqrt(jnp.mean(o * o, axis=-1, keepdims=True) + 1e-6)
        yb[:, h * W : (h + 1) * W] = (o * sg[:, h * W : (h + 1) * W]).astype(BF)
    l_wo.wait()
    cw = D // NCH
    c_c = []
    for n in range(NCH):
        part = mm(yb[...], wo[:, n * cw : (n + 1) * cw]).astype(BF)
        for k in range(2 * NY):
            pm[n, k % 2, k // 2] = part[k * 16 : (k + 1) * 16]
        c_c.append(send(15 + n, pm.at[n, 1 - co], rc.at[n], rs_c.at[n], partner))
    c_y = []
    for n in range(NCH):
        c_c[n].wait_recv()
        s2[n] = (pm[n, co].astype(F32) + rc[n].astype(F32)).astype(BF)
        c_y.append([
            send(15 + NCH + 3 * n + d - 1, s2.at[n, lax.rem(y + d, NY)], ry.at[n, d - 1], rs_y.at[n, d - 1], at_y(d))
            for d in (1, 2, 3)
        ])
    for n in range(NCH):
        for cp in c_y[n]:
            cp.wait_recv()
        tot = pm[n, co, y].astype(F32) + rc[n, y].astype(F32)
        for d in range(3):
            tot = tot + ry[n, d].astype(F32)
        out_ref[:, n * cw : (n + 1) * cw] = tot.astype(BF)
    for cond, cp in sends:
        if cond is None:
            cp.wait_send()
        else:
            pl.when(cond)(cp.wait_send)


def per_device(*args):
    vm = pltpu.VMEM
    dma = pltpu.SemaphoreType.DMA
    any_spec = pl.BlockSpec(memory_space=pl.ANY)
    return pl.pallas_call(
        kernel,
        out_shape=pltpu.VMEM((16, D), BF),
        in_specs=[any_spec] * 13,
        out_specs=pl.BlockSpec(memory_space=pltpu.VMEM),
        scratch_shapes=[
            vm((T, D), BF), vm((D, 256), BF), vm((D, 256), BF), vm((D, 512), BF), vm((D, 512), BF),
            vm((512, D), BF), vm((4, 256), BF), vm((4, 256), BF), vm((4, 512), BF),
            vm((HV, T), F32), vm((HV, T), F32), pltpu.SMEM((DOCS,), jnp.int32), pltpu.SMEM((HV,), F32),
            vm((T, 256), BF), vm((T, 256), BF), vm((T, 512), BF),
            vm((16, 256), BF), vm((16, 256), BF), vm((16, 512), BF),
            vm((T + 8, 1024), F32), vm((2 * HV, T), F32),
            vm((HV, T, T), F32), vm((HV, T, T), F32), vm((HV, T, T), F32), vm((HV, T, T), F32),
            vm((T, (SUB - 1) * T), BF),
            vm((T, 512), F32),
            vm((HV, W, 2 * W), BF), vm((2, NX, W, 2 * W), BF),
            vm((HV, T, W), F32), vm((HV, T, W), BF),
            vm((2, W, W), BF), vm((2, W, W), BF), vm((W, W), BF),
            vm((NX, W, W), BF), vm((HV, W, W), BF),
            vm((T, 512), BF),
            vm((NCH, 2, NY, 16, D // NCH), BF), vm((NCH, NY, 16, D // NCH), BF),
            vm((NCH, NY, 16, D // NCH), BF), vm((NCH, 3, 16, D // NCH), BF),
            pltpu.SemaphoreType.REGULAR((NX,)), pltpu.SemaphoreType.REGULAR,
            dma((13,)), dma((16 + NCH * 4,)), dma((3,)), dma((3,)), dma((4,)), dma((3,)), dma((3,)),
            dma((NCH,)), dma((NCH, 3)),
        ],
        name="layer",
        compiler_params=pltpu.CompilerParams(
            collective_id=0, has_side_effects=True, vmem_limit_bytes=56 << 20
        ),
    )(*args)


def solution(mesh):
    in_specs = (
        P("ctx", None),
        P(),
        P(None, "head"),
        P(None, "head"),
        P(None, "head"),
        P(None, "head"),
        P(None, "head"),
        P(None, "head"),
        P(None, "head"),
        P("head", "ctx"),
        P("head", "ctx"),
        P("head"),
        P("head", None),
    )
    out_specs = P(("ctx", "head"), None)
    return jax.shard_map(
        per_device, mesh=mesh, in_specs=in_specs, out_specs=out_specs, check_vma=False
    )
```
